32 devices in a mesh: dp: 32 (over z, y, x, core).
Axes of the slice: x: 2, y: 2, z: 4, core: 2. Of those that a mesh axis runs over, the one named last changes fastest.
Arguments:
- tokens: bfloat16 [64, 512, 512], P('dp'), may hold values from -6 to 6
- memory: bfloat16 [64, 512, 512], P('dp'), may hold values from -6 to 6
- segments: int32 [64, 512], P('dp'), may hold values from 0 to 3, never falling along the last dimension, each value on 1 to 256 neighbouring positions
- cotangent: bfloat16 [64, 512, 512], P('dp'), may hold values from -6 to 6
- group_sizes: int32 [8], replicated, may hold values from 1 to 8, 32 in all
- task_embed: bfloat16 [8, 64], replicated, may hold values from -4 to 4
- position_embed: bfloat16 [2, 64], replicated, may hold values from -4 to 4
- hyper_first: bfloat16 [64, 128], replicated, may hold values from -0.75 to 0.75
- hyper_second: bfloat16 [128, 64], replicated, may hold values from -0.5 to 0.5
- hyper_gain: bfloat16 [64, 1536], replicated, may hold values from -0.375 to 0.375
- hyper_down: bfloat16 [64, 8192], replicated, may hold values from -0.03125 to 0.03125
- hyper_up: bfloat16 [64, 8192], replicated, may hold values from -0.1875 to 0.1875
- self_qkv: bfloat16 [3, 512, 512], replicated, may hold values from -0.25 to 0.25
- self_out: bfloat16 [512, 512], replicated, may hold values from -0.75 to 0.75
- cross_qkv: bfloat16 [3, 512, 512], replicated, may hold values from -0.25 to 0.25
- cross_out: bfloat16 [512, 512], replicated, may hold values from -1.5 to 1.5
- ffn_in: bfloat16 [512, 2048], replicated, may hold values from -0.25 to 0.25
- ffn_out: bfloat16 [2048, 512], replicated, may hold values from -0.125 to 0.125
Outputs:
- output: bfloat16 [64, 512, 512], P('dp')
- input_grad: float32 [64, 512, 512], P('dp')
- memory_grad: float32 [64, 512, 512], P('dp')
- task_grad: float32 [8, 64], replicated
- position_grad: float32 [2, 64], replicated
- hyper_first_grad: float32 [64, 128], replicated
- hyper_second_grad: float32 [128, 64], replicated
- hyper_gain_grad: float32 [64, 1536], replicated
- hyper_down_grad: float32 [64, 8192], replicated
- hyper_up_grad: float32 [64, 8192], replicated
- self_qkv_grad: float32 [3, 512, 512], replicated
- self_out_grad: float32 [512, 512], replicated
- cross_qkv_grad: float32 [3, 512, 512], replicated
- cross_out_grad: float32 [512, 512], replicated
- ffn_in_grad: float32 [512, 2048], replicated
- ffn_out_grad: float32 [2048, 512], replicated
The draws below stay inside these ranges and needn't reach their ends.
Inputs may be any that keep to these rules, and one draw needn't show every extreme that they name: The devices of dp belong to tasks in order: the first group_sizes[0] devices to task 0, the next group_sizes[1] to task 1, and so on; the sizes add up to 32. `segments`: along each row the segment numbers never fall; every segment holds at most 256 positions.
All inputs are finite; a program needn't handle non-finite values.
Results may differ from the reference program's by a relative error of at most 0.024.
Values sent between devices are 32-bit elements; how exact they have to be, the bound alone decides.
No kernel may reach another device: no remote copies, remote signals or barrier semaphores. Data moves between devices by JAX's collectives and lax.ppermute only.
A program may use at most 192 MiB of HBM per device.

```python
import math
import jax
import jax.numpy as jnp
import numpy as np
from jax import lax

D = 512
HEADS = 8
HEAD_DIM = 64
FF = 2048
RANK = 16
EMB = 64
HYPER = 128
NTASK = 8
SEQ = 512
MEM = 512
ROWS_DEV = 2
WORKERS = 32
ROWS = 64


def shard_levels(rng, extent, pieces, smallest, high):
    def one(position, parts):
        steps = jax.random.uniform(jax.random.fold_in(jax.random.fold_in(rng, 6), position), (parts,), jnp.float32, smallest / len(pieces), high / len(pieces))
        return jnp.repeat(jnp.exp(steps), extent[position] // parts).reshape((-1,) + (1,) * (len(extent) - position - 1))

    factor_of = one(*pieces[0])
    for cut in pieces[1:]:
        factor_of = factor_of * one(*cut)
    return factor_of


def length_profile(amount, total, limit, lean):
    loads = [(1 << 20) // math.isqrt(grade ** lean) + 1 for grade in range(2, amount + 1)]
    spare, given = total - limit - (amount - 1), [1] * (amount - 1)
    while spare > 0:
        free = [i for i in range(amount - 1) if given[i] < limit]
        mass, budget = sum([loads[i] for i in free]), spare
        for i in free:
            addition = min(limit - given[i], max(1, budget * loads[i] // mass), spare)
            given[i] = given[i] + addition
            spare = spare - addition
    return np.array([limit] + given)


def ragged(key, count, total, bound, skew):
    if count == 2:
        one = jax.random.randint(key, (), max(1, total - bound), min(bound, total - 1) + 1)
        return jnp.stack([one, total - one])
    tallies = jnp.asarray(length_profile(count, total, bound, skew), jnp.int32)
    couples = (count - 1) // 2
    giver, receiver = tallies[1:1 + 2 * couples:2], tallies[2:2 + 2 * couples:2]
    margin = jnp.minimum(giver - 1, bound - receiver)
    shifted = jax.random.randint(jax.random.fold_in(key, 1), (couples,), 0, 1 << 20) % (margin + 1)
    tallies = tallies.at[1:1 + 2 * couples:2].set(giver - shifted).at[2:2 + 2 * couples:2].set(receiver + shifted)
    return tallies[jax.random.permutation(jax.random.fold_in(key, 2), count)]


def centred(key, shape, scale, reach, cuts=(), dtype=jnp.bfloat16):
    values = jax.random.normal(key, shape, jnp.float32) * scale
    if len(cuts) > 0:
        values = shard_levels(key, shape, cuts, -0.22, 0.18) * values
    return jnp.clip(values, min=-reach, max=reach).astype(dtype)


def setup_inputs(seed: int = 0) -> dict:
    splits = jax.random.split(jax.random.key(seed), 19)
    return {
        "tokens": centred(splits[0], (ROWS, SEQ, D), 1.0, 6.0, ((0, 32),)),
        "memory": centred(splits[1], (ROWS, MEM, D), 1.0, 6.0, ((0, 32),)),
        "segments": jax.vmap(lambda own: jnp.searchsorted(jnp.cumsum(ragged(own, 4, SEQ, SEQ // 2, 0)), jnp.arange(SEQ), side="right"))(jax.random.split(splits[2], ROWS)).reshape((ROWS, SEQ)).astype(jnp.int32),
        "cotangent": centred(splits[3], (ROWS, SEQ, D), 1.0, 6.0, ((0, 32),)),
        "group_sizes": ragged(splits[4], NTASK, WORKERS, WORKERS // 4, 2).astype(jnp.int32),
        "task_embed": centred(splits[5], (NTASK, EMB), 1.0, 4.0),
        "position_embed": centred(splits[6], (2, EMB), 1.0, 4.0),
        "hyper_first": centred(splits[7], (EMB, HYPER), EMB ** -0.5, 0.75),
        "hyper_second": centred(splits[8], (HYPER, EMB), HYPER ** -0.5, 0.5),
        "hyper_gain": centred(splits[9], (EMB, 3 * D), (EMB * 4) ** -0.5, 0.375),
        "hyper_down": centred(splits[10], (EMB, D * RANK), (EMB * D) ** -0.5, 0.03125),
        "hyper_up": centred(splits[11], (EMB, RANK * D), (EMB * RANK) ** -0.5, 0.1875),
        "self_qkv": centred(splits[12], (3, D, D), D ** -0.5, 0.25),
        "self_out": centred(splits[13], (D, D), (D // 8) ** -0.5, 0.75),
        "cross_qkv": centred(splits[14], (3, D, D), D ** -0.5, 0.25),
        "cross_out": centred(splits[15], (D, D), (D // 32) ** -0.5, 1.5),
        "ffn_in": centred(splits[16], (D, FF), D ** -0.5, 0.25),
        "ffn_out": centred(splits[17], (FF, D), FF ** -0.5, 0.125),
    }


epsilon = 1e-06
highest = lax.Precision.HIGHEST

@jax.custom_vjp
def low(v):
    return lax.optimization_barrier(v.astype(jnp.bfloat16)).astype(jnp.float32)

@jax.custom_vjp
def low_back(v):
    return v

def low_keep(v):
    return (low(v), None)

def low_pass(kept, grad):
    return (grad,)

def back_keep(v):
    return (v, None)

def back_low(kept, grad):
    return (low(grad),)
low.defvjp(low_keep, low_pass)
low_back.defvjp(back_keep, back_low)

def rms_scale(values, gain_vec):
    return values * lax.rsqrt(lax.optimization_barrier(jnp.mean(values * values, axis=-1, keepdims=True)) + epsilon) * gain_vec

def product(left, right):
    return jnp.dot(left, right, precision=highest)

def attention(queries, key_rows, value_rows, allowed, masked):
    head_q = queries.reshape(queries.shape[0], HEADS, HEAD_DIM)
    head_k = key_rows.reshape(key_rows.shape[0], HEADS, HEAD_DIM)
    head_v = value_rows.reshape(value_rows.shape[0], HEADS, HEAD_DIM)
    scores = low_back(jnp.einsum('qhd,khd->hqk', head_q, head_k, precision=highest) * HEAD_DIM ** (-0.5))
    if masked:
        scores = jnp.where(allowed[None], scores, -1000000000.0)
    probs = low(jax.nn.softmax(scores, axis=-1))
    mixed = jnp.einsum('hqk,khd->qhd', probs, head_v, precision=highest)
    return mixed.reshape(queries.shape[0], HEADS * HEAD_DIM)

def hyper_tables(params):
    task_embed, position_embed, hyper_first, hyper_second, hyper_gain, hyper_down, hyper_up = params[:7]
    hidden = jax.nn.silu(product(task_embed, hyper_first))
    code = product(hidden, hyper_second)
    gains = 1.0 + product(code, hyper_gain).reshape(NTASK, 3, D)
    codes = code[:, None, :] + position_embed[None, :, :]
    downs = low(jnp.einsum('tpe,ek->tpk', codes, hyper_down, precision=highest).reshape(NTASK, 2, D, RANK))
    ups = low(jnp.einsum('tpe,ek->tpk', codes, hyper_up, precision=highest).reshape(NTASK, 2, RANK, D))
    return (gains, downs, ups)

def layer_row(weights, gain_rows, down_rows, up_rows, token_row, mem_row, allowed):
    self_qkv, self_out, cross_qkv, cross_out, ffn_in, ffn_out = weights
    in_one = low(rms_scale(token_row, gain_rows[0]))
    self_parts = [low_back(low(product(in_one, self_qkv[index]))) for index in range(3)]
    mixed_one = low_back(low(attention(self_parts[0], self_parts[1], self_parts[2], allowed, True)))
    branch = low_back(product(mixed_one, self_out))
    narrow = low_back(product(low(branch), down_rows[0]))
    widen = low_back(product(low(jax.nn.silu(narrow)), up_rows[0]))
    after_one = token_row + branch + widen
    in_two = low(rms_scale(after_one, gain_rows[1]))
    query_two = low_back(low(product(in_two, cross_qkv[0])))
    key_two = low_back(low(product(mem_row, cross_qkv[1])))
    value_two = low_back(low(product(mem_row, cross_qkv[2])))
    mixed_two = low_back(low(attention(query_two, key_two, value_two, allowed, False)))
    cross = low_back(product(mixed_two, cross_out))
    after_two = after_one + cross
    in_three = low(rms_scale(after_two, gain_rows[2]))
    inner = low_back(product(in_three, ffn_in))
    outer = low_back(product(low(jax.nn.gelu(inner, approximate=False)), ffn_out))
    narrow_two = low_back(product(low(outer), down_rows[1]))
    widen_two = low_back(product(low(jax.nn.silu(narrow_two)), up_rows[1]))
    return after_two + outer + widen_two

def forward(tokens_f, memory_f, params, segments, row_task):
    gains_all, downs, ups = hyper_tables(params)
    weights = params[7:]
    positions = jnp.arange(SEQ)
    causal = positions[:, None] >= positions[None, :]

    def step(carry, item):
        token_row, mem_row, seg_row, task_now = item
        allowed = causal & (seg_row[:, None] == seg_row[None, :])
        result = layer_row(weights, gains_all[task_now], downs[task_now], ups[task_now], token_row, mem_row, allowed)
        return (carry, result)
    _, outputs = lax.scan(jax.checkpoint(step), jnp.zeros((), jnp.float32), (tokens_f, memory_f, segments, row_task))
    return outputs

def reference(tokens, memory, segments, cotangent, group_sizes, task_embed, position_embed, hyper_first, hyper_second, hyper_gain, hyper_down, hyper_up, self_qkv, self_out, cross_qkv, cross_out, ffn_in, ffn_out):
    ends = jnp.cumsum(group_sizes).astype(jnp.int32)
    owner = (jnp.arange(ROWS) // ROWS_DEV).astype(jnp.int32)
    row_task = lax.optimization_barrier(jnp.sum((ends[None, :] <= owner[:, None]).astype(jnp.int32), axis=1)).astype(jnp.int32)
    row_weight = WORKERS / (NTASK * group_sizes[row_task].astype(jnp.float32))
    params = tuple((item.astype(jnp.float32) for item in (task_embed, position_embed, hyper_first, hyper_second, hyper_gain, hyper_down, hyper_up, self_qkv, self_out, cross_qkv, cross_out, ffn_in, ffn_out)))

    def wrapped(tokens_f, memory_f, params_f):
        return forward(tokens_f, memory_f, params_f, segments, row_task)
    result, pullback = jax.vjp(wrapped, tokens.astype(jnp.float32), memory.astype(jnp.float32), params)
    grad_tokens, grad_memory, grad_params = pullback(cotangent.astype(jnp.float32) * row_weight[:, None, None])
    return (result.astype(jnp.bfloat16), grad_tokens, grad_memory, grad_params[0], grad_params[1], grad_params[2], grad_params[3], grad_params[4], grad_params[5], grad_params[6], grad_params[7], grad_params[8], grad_params[9], grad_params[10], grad_params[11], grad_params[12])
```

```python
import jax
import jax.numpy as jnp
from jax import lax
from jax.sharding import PartitionSpec as P

HEADS = 8
HEAD_DIM = 64


epsilon = 1e-06
highest = lax.Precision.HIGHEST


def rms_scale(values, gain_vec):
    return (
        values * lax.rsqrt(jnp.mean(values * values, axis=-1, keepdims=True) + epsilon) * gain_vec
    )


def matmul(left, right):
    return jnp.dot(left, right, preferred_element_type=jnp.float32)


def left_matmul(left, right):
    return lax.dot_general(
        left, right, (((0,), (0,)), ((), ())), preferred_element_type=jnp.float32
    )


def right_matmul(left, right):
    return lax.dot_general(
        left, right, (((1,), (1,)), ((), ())), preferred_element_type=jnp.float32
    )


def split_heads(values):
    return values.reshape(values.shape[0], values.shape[1], HEADS, HEAD_DIM)


def head_scores(head_q, head_k, allowed, masked):
    scores = jnp.einsum(
        "bqhd,bkhd->bhqk", head_q, head_k, preferred_element_type=jnp.float32
    ) * HEAD_DIM ** (-0.5)
    if masked:
        scores = jnp.where(allowed[:, None], scores, -1000000000.0)
    return scores


def attend(queries, key_rows, value_rows, allowed, masked):
    scores = head_scores(split_heads(queries), split_heads(key_rows), allowed, masked)
    top_score = jnp.max(scores, axis=-1, keepdims=True)
    expo = jnp.exp(scores - top_score)
    totals = jnp.sum(expo, axis=-1, keepdims=True)
    probs = (expo / totals).astype(jnp.bfloat16)
    mixed = jnp.einsum(
        "bhqk,bkhd->bqhd", probs, split_heads(value_rows), preferred_element_type=jnp.float32
    )
    return (mixed.reshape(queries.shape).astype(jnp.bfloat16), top_score + jnp.log(totals))


def attend_back(queries, key_rows, value_rows, allowed, masked, logsum, grad_mixed):
    head_q = split_heads(queries)
    head_k = split_heads(key_rows)
    head_v = split_heads(value_rows)
    head_g = split_heads(grad_mixed)
    probs = jnp.exp(head_scores(head_q, head_k, allowed, masked) - logsum)
    grad_probs = jnp.einsum("bqhd,bkhd->bhqk", head_g, head_v, preferred_element_type=jnp.float32)
    grad_values = jnp.einsum(
        "bhqk,bqhd->bkhd", probs.astype(jnp.bfloat16), head_g, preferred_element_type=jnp.float32
    )
    delta = jnp.sum(probs * grad_probs, axis=-1, keepdims=True)
    grad_scores = (probs * (grad_probs - delta)).astype(jnp.bfloat16)
    scale_now = HEAD_DIM ** (-0.5)
    grad_queries = (
        jnp.einsum("bhqk,bkhd->bqhd", grad_scores, head_k, preferred_element_type=jnp.float32)
        * scale_now
    )
    grad_keys = (
        jnp.einsum("bhqk,bqhd->bkhd", grad_scores, head_q, preferred_element_type=jnp.float32)
        * scale_now
    )
    return (
        grad_queries.reshape(queries.shape).astype(jnp.bfloat16),
        grad_keys.reshape(key_rows.shape).astype(jnp.bfloat16),
        grad_values.reshape(value_rows.shape).astype(jnp.bfloat16),
    )


def silu_back(values, grad_out):
    return jax.vjp(jax.nn.silu, values)[1](grad_out)[0]


ORDER_A = ((1, 1), (2, 4), (4, 2), (8, 8), (16, 16))
ORDER_B = ((1, 1), (2, 4), (8, 8), (16, 16), (4, 2))


def all_sum(total, order):
    devices = lax.axis_size("dp")
    place = lax.axis_index("dp")

    def swap(values, even_bit, odd_bit):
        moves = [(i, i ^ (odd_bit if i % 2 else even_bit)) for i in range(devices)]
        return lax.ppermute(values, "dp", moves)

    def upper(even_bit, odd_bit):
        return jnp.where(place % 2 == 1, (place // odd_bit) % 2, (place // even_bit) % 2)

    for even_bit, odd_bit in order:
        half = total.shape[0] // 2
        side = upper(even_bit, odd_bit)
        sent = lax.dynamic_slice_in_dim(total, (1 - side) * half, half)
        kept = lax.dynamic_slice_in_dim(total, side * half, half)
        total = kept + swap(sent, even_bit, odd_bit)
    high = 32
    while high < devices:
        total = total + swap(total, high, high)
        high *= 2
    for even_bit, odd_bit in order[::-1]:
        side = upper(even_bit, odd_bit)
        other = swap(total, even_bit, odd_bit)
        total = jnp.concatenate(
            [jnp.where(side == 0, total, other), jnp.where(side == 0, other, total)]
        )
    return total


def on_device(
    tokens,
    memory,
    segments,
    cotangent,
    group_sizes,
    task_embed,
    position_embed,
    hyper_first,
    hyper_second,
    hyper_gain,
    hyper_down,
    hyper_up,
    self_qkv,
    self_out,
    cross_qkv,
    cross_out,
    ffn_in,
    ffn_out,
):
    row_count, seq_len, model_width = tokens.shape
    mem_len = memory.shape[1]
    token_count = row_count * seq_len
    devices = lax.axis_size("dp")
    place = lax.axis_index("dp")
    ntask = group_sizes.shape[0]
    emb_width = task_embed.shape[1]
    ends = jnp.cumsum(group_sizes)
    task_now = jnp.sum((ends <= place).astype(jnp.int32))
    onehot = (jnp.arange(ntask) == task_now).astype(jnp.float32)
    share = devices / (ntask * jnp.sum(onehot * group_sizes.astype(jnp.float32)))
    table = task_embed.astype(jnp.float32)
    first_f = hyper_first.astype(jnp.float32)
    second_f = hyper_second.astype(jnp.float32)
    gain_f = hyper_gain.astype(jnp.float32)
    down_f = hyper_down.astype(jnp.float32)
    up_f = hyper_up.astype(jnp.float32)
    position_f = position_embed.astype(jnp.float32)
    embed = jnp.dot(onehot, table, precision=highest)
    pre_act = jnp.dot(embed, first_f, precision=highest)
    hidden = jax.nn.silu(pre_act)
    code = jnp.dot(hidden, second_f, precision=highest)
    gains = 1.0 + jnp.dot(code, gain_f, precision=highest).reshape(3, model_width)
    codes = code[None, :] + position_f
    down_w = (
        jnp.dot(codes, down_f, precision=highest).reshape(2, model_width, -1).astype(jnp.bfloat16)
    )
    up_w = jnp.dot(codes, up_f, precision=highest).reshape(2, -1, model_width).astype(jnp.bfloat16)
    flat_x = tokens.reshape(token_count, model_width).astype(jnp.float32)
    mem_flat = memory.reshape(row_count * mem_len, model_width)
    positions = jnp.arange(seq_len)
    allowed = (segments[:, :, None] == segments[:, None, :]) & (
        positions[:, None] >= positions[None, :]
    )[None]
    row_shape = (row_count, seq_len, model_width)
    mem_shape = (row_count, mem_len, model_width)
    in_one = rms_scale(flat_x, gains[0]).astype(jnp.bfloat16)
    self_parts = jnp.einsum(
        "nd,jde->jne", in_one, self_qkv, preferred_element_type=jnp.float32
    ).astype(jnp.bfloat16)
    self_q = self_parts[0].reshape(row_shape)
    self_k = self_parts[1].reshape(row_shape)
    self_v = self_parts[2].reshape(row_shape)
    mixed_one, logsum_one = attend(self_q, self_k, self_v, allowed, True)
    mixed_one = mixed_one.reshape(token_count, model_width)
    branch = matmul(mixed_one, self_out)
    branch_low = branch.astype(jnp.bfloat16)
    narrow = matmul(branch_low, down_w[0])
    narrow_act = jax.nn.silu(narrow).astype(jnp.bfloat16)
    after_one = flat_x + branch + matmul(narrow_act, up_w[0])
    in_two = rms_scale(after_one, gains[1]).astype(jnp.bfloat16)
    query_two = matmul(in_two, cross_qkv[0]).astype(jnp.bfloat16).reshape(row_shape)
    mem_parts = jnp.einsum(
        "nd,jde->jne", mem_flat, cross_qkv[1:], preferred_element_type=jnp.float32
    ).astype(jnp.bfloat16)
    key_two = mem_parts[0].reshape(mem_shape)
    value_two = mem_parts[1].reshape(mem_shape)
    mixed_two, logsum_two = attend(query_two, key_two, value_two, allowed, False)
    mixed_two = mixed_two.reshape(token_count, model_width)
    after_two = after_one + matmul(mixed_two, cross_out)
    in_three = rms_scale(after_two, gains[2]).astype(jnp.bfloat16)
    inner = matmul(in_three, ffn_in)
    inner_act = jax.nn.gelu(inner, approximate=False).astype(jnp.bfloat16)
    outer = matmul(inner_act, ffn_out)
    outer_low = outer.astype(jnp.bfloat16)
    narrow_two = matmul(outer_low, down_w[1])
    narrow_two_act = jax.nn.silu(narrow_two).astype(jnp.bfloat16)
    result = after_two + outer + matmul(narrow_two_act, up_w[1])
    output = result.astype(jnp.bfloat16).reshape(row_shape)
    grad_now = cotangent.reshape(token_count, model_width).astype(jnp.float32) * share
    grad_low = grad_now.astype(jnp.bfloat16)
    up_grad_two = left_matmul(narrow_two_act, grad_low)
    d_narrow_two = silu_back(narrow_two, right_matmul(grad_low, up_w[1])).astype(jnp.bfloat16)
    down_grad_two = left_matmul(outer_low, d_narrow_two)
    d_outer = (grad_now + right_matmul(d_narrow_two, down_w[1])).astype(jnp.bfloat16)
    ffn_out_grad = left_matmul(inner_act, d_outer)
    gelu_pull = jax.vjp(lambda values: jax.nn.gelu(values, approximate=False), inner)[1]
    d_inner = gelu_pull(right_matmul(d_outer, ffn_out))[0].astype(jnp.bfloat16)
    ffn_in_grad = left_matmul(in_three, d_inner)
    norm_pull = jax.vjp(rms_scale, after_two, gains[2])[1]
    d_after, gain_grad_three = norm_pull(right_matmul(d_inner, ffn_in))
    grad_now = grad_now + d_after
    grad_low = grad_now.astype(jnp.bfloat16)
    cross_out_grad = left_matmul(mixed_two, grad_low)
    d_mixed_two = right_matmul(grad_low, cross_out).astype(jnp.bfloat16).reshape(row_shape)
    d_query_two, d_key_two, d_value_two = attend_back(
        query_two, key_two, value_two, allowed, False, logsum_two, d_mixed_two
    )
    d_query_two = d_query_two.reshape(token_count, model_width)
    d_key_two = d_key_two.reshape(row_count * mem_len, model_width)
    d_value_two = d_value_two.reshape(row_count * mem_len, model_width)
    cross_qkv_grad = jnp.stack(
        [
            left_matmul(in_two, d_query_two),
            left_matmul(mem_flat, d_key_two),
            left_matmul(mem_flat, d_value_two),
        ]
    )
    memory_grad = right_matmul(d_key_two, cross_qkv[1]) + right_matmul(d_value_two, cross_qkv[2])
    norm_pull = jax.vjp(rms_scale, after_one, gains[1])[1]
    d_after, gain_grad_two = norm_pull(right_matmul(d_query_two, cross_qkv[0]))
    grad_now = grad_now + d_after
    grad_low = grad_now.astype(jnp.bfloat16)
    up_grad_one = left_matmul(narrow_act, grad_low)
    d_narrow = silu_back(narrow, right_matmul(grad_low, up_w[0])).astype(jnp.bfloat16)
    down_grad_one = left_matmul(branch_low, d_narrow)
    d_branch = (grad_now + right_matmul(d_narrow, down_w[0])).astype(jnp.bfloat16)
    self_out_grad = left_matmul(mixed_one, d_branch)
    d_mixed_one = right_matmul(d_branch, self_out).astype(jnp.bfloat16).reshape(row_shape)
    d_self = attend_back(self_q, self_k, self_v, allowed, True, logsum_one, d_mixed_one)
    d_stack = jnp.stack([part.reshape(token_count, model_width) for part in d_self])
    self_qkv_grad = jnp.einsum("nd,jne->jde", in_one, d_stack, preferred_element_type=jnp.float32)
    d_in_one = jnp.einsum("jne,jde->nd", d_stack, self_qkv, preferred_element_type=jnp.float32)
    norm_pull = jax.vjp(rms_scale, flat_x, gains[0])[1]
    d_x, gain_grad_one = norm_pull(d_in_one)
    input_grad = (grad_now + d_x).reshape(row_shape)
    down_grads = jnp.stack([down_grad_one.reshape(-1), down_grad_two.reshape(-1)])
    up_grads = jnp.stack([up_grad_one.reshape(-1), up_grad_two.reshape(-1)])
    gain_grads = jnp.concatenate([gain_grad_one, gain_grad_two, gain_grad_three])
    d_codes = jnp.dot(down_grads, down_f.T, precision=highest) + jnp.dot(
        up_grads, up_f.T, precision=highest
    )
    d_code = jnp.sum(d_codes, axis=0) + jnp.dot(gain_f, gain_grads, precision=highest)
    own_second = jnp.outer(hidden, d_code)
    d_pre = silu_back(pre_act, jnp.dot(second_f, d_code, precision=highest))
    own_first = jnp.outer(embed, d_pre)
    own_task = jnp.outer(onehot, jnp.dot(first_f, d_pre, precision=highest))
    spread = onehot[:, None, None]
    small_parts = [
        (spread * down_grads[None]).reshape(-1),
        (spread * up_grads[None]).reshape(-1),
        (onehot[:, None] * gain_grads[None]).reshape(-1),
        own_first.reshape(-1),
        own_second.reshape(-1),
        d_codes.reshape(-1),
        own_task.reshape(-1),
    ]
    small_flat = jnp.concatenate(small_parts)
    unit = 8 * 32 * model_width
    pad = (-small_flat.shape[0]) % unit
    small_flat = jnp.concatenate([small_flat, jnp.zeros((pad,), jnp.float32)])
    sum_out = all_sum(ffn_out_grad, ORDER_A)
    sum_in = all_sum(ffn_in_grad, ORDER_B)
    cross_rows = jnp.concatenate([cross_out_grad[None], cross_qkv_grad]).reshape(-1, model_width)
    sum_cross = all_sum(cross_rows, ORDER_A).reshape(4, model_width, model_width)
    self_rows = jnp.concatenate([self_out_grad[None], self_qkv_grad]).reshape(-1, model_width)
    sum_self = all_sum(self_rows, ORDER_B).reshape(4, model_width, model_width)
    sum_small = all_sum(small_flat.reshape(-1, model_width), ORDER_A).reshape(-1)
    sums, at = [], 0
    for part in small_parts:
        sums.append(sum_small[at : at + part.shape[0]])
        at += part.shape[0]
    every_hidden = jax.nn.silu(jnp.dot(table, first_f, precision=highest))
    every_code = jnp.dot(every_hidden, second_f, precision=highest)
    every_codes = (every_code[:, None, :] + position_f[None]).reshape(-1, emb_width)
    hyper_down_grad = jnp.dot(every_codes.T, sums[0].reshape(2 * ntask, -1), precision=highest)
    hyper_up_grad = jnp.dot(every_codes.T, sums[1].reshape(2 * ntask, -1), precision=highest)
    hyper_gain_grad = jnp.dot(every_code.T, sums[2].reshape(ntask, -1), precision=highest)
    return (
        output,
        input_grad,
        memory_grad.reshape(mem_shape),
        sums[6].reshape(ntask, emb_width),
        sums[5].reshape(2, emb_width),
        sums[3].reshape(hyper_first.shape),
        sums[4].reshape(hyper_second.shape),
        hyper_gain_grad,
        hyper_down_grad,
        hyper_up_grad,
        sum_self[1:],
        sum_self[0],
        sum_cross[1:],
        sum_cross[0],
        sum_in,
        sum_out,
    )


def solution(mesh):
    placed = (
        P("dp", None, None),
        P("dp", None, None),
        P("dp", None),
        P("dp", None, None),
        P(),
        P(),
        P(),
        P(),
        P(),
        P(),
        P(),
        P(),
        P(),
        P(),
        P(),
        P(),
        P(),
        P(),
    )
    return jax.shard_map(
        on_device,
        mesh=mesh,
        in_specs=placed,
        out_specs=(
            P("dp", None, None),
            P("dp", None, None),
            P("dp", None, None),
            P(),
            P(),
            P(),
            P(),
            P(),
            P(),
            P(),
            P(),
            P(),
            P(),
            P(),
            P(),
            P(),
        ),
        check_vma=False,
    )
```

```python
import functools

import jax
import jax.numpy as jnp
from jax import lax
from jax.experimental import pallas as pl
from jax.experimental.pallas import tpu as pltpu
from jax.sharding import PartitionSpec as P

PAIRS = 4
LANES = 128
RANK = 16
LOG2E = 1.4426950408889634
epsilon = 1e-06
highest = lax.Precision.HIGHEST
f32 = jnp.float32
bf16 = jnp.bfloat16


def dot(left, right):
    return jnp.dot(left, right, preferred_element_type=f32)


def dot_nt(left, right):
    return lax.dot_general(left, right, (((1,), (1,)), ((), ())), preferred_element_type=f32)


def dot_tn(left, right):
    return lax.dot_general(left, right, (((0,), (0,)), ((), ())), preferred_element_type=f32)


def three(values):
    high = values.astype(bf16)
    rest = values - high.astype(f32)
    mid = rest.astype(bf16)
    return high, mid, (rest - mid.astype(f32)).astype(bf16)


def dot_exact(values, table):
    high, mid, low = three(values)
    return dot(high, table) + (dot(mid, table) + dot(low, table))


def dot_exact_nt(values, table):
    high, mid, low = three(values)
    return dot_nt(high, table) + (dot_nt(mid, table) + dot_nt(low, table))


def rms_back(values, inv, gain, grad):
    unit = values * inv
    scaled = grad * gain
    mean = jnp.mean(scaled * unit, axis=-1, keepdims=True)
    return inv * (scaled - unit * mean), jnp.sum(grad * unit, axis=0, keepdims=True)


def rms_inv(values):
    return lax.rsqrt(jnp.mean(values * values, axis=-1, keepdims=True) + epsilon)


def low_lanes():
    return lax.broadcasted_iota(jnp.int32, (1, LANES), 1) < 64


def silu_back(values, grad):
    gate = lax.logistic(values)
    return grad * (gate * (1.0 + values * (1.0 - gate)))


def task_place(sizes_ref, count, place):
    end, task = jnp.int32(0), jnp.int32(0)
    for i in range(count):
        end = end + sizes_ref[i]
        task = task + jnp.where(end <= place, 1, 0)
    size = sizes_ref[0]
    for i in range(1, count):
        size = jnp.where(task == i, sizes_ref[i], size)
    return task, size


def pick_row(table, task):
    rows = lax.broadcasted_iota(jnp.int32, table.shape, 0)
    return jnp.sum(jnp.where(rows == task, table, 0.0), axis=0, keepdims=True)


def fold_tables():
    feature = lax.broadcasted_iota(jnp.int32, (512, 64), 0)
    block = lax.broadcasted_iota(jnp.int32, (512, 64), 1)
    expand = jnp.where(feature // 8 == block, 1.0, 0.0).astype(bf16)
    feature = lax.broadcasted_iota(jnp.int32, (512, LANES), 0)
    lane = lax.broadcasted_iota(jnp.int32, (512, LANES), 1)
    own = (lane // RANK) == (feature % 8)
    row = lax.broadcasted_iota(jnp.int32, (LANES, LANES), 0)
    lane = lax.broadcasted_iota(jnp.int32, (LANES, LANES), 1)
    fold = jnp.where((row % RANK) == lane, 1.0, 0.0).astype(bf16)
    return expand, own, fold


def attend_block(pair_q, keys, values_ones, bias):
    low = low_lanes()
    probs, mixed = [], []
    for head in range(2):
        own = low if head == 0 else jnp.logical_not(low)
        scores = dot_nt(jnp.where(own, pair_q, jnp.zeros_like(pair_q)), keys)
        if bias is not None:
            scores = scores + bias
        top = jnp.max(scores, axis=-1, keepdims=True)
        prob = jnp.exp2((scores - top) * LOG2E).astype(bf16)
        probs.append(prob)
        mixed.append(dot(prob, values_ones))
    total = jnp.where(low, mixed[0][:, LANES:], mixed[1][:, LANES:])
    share = 1.0 / total
    out = jnp.where(low, mixed[0][:, :LANES], mixed[1][:, :LANES]) * share
    return probs, out.astype(bf16), share


def hyper_tables(task, embed_ref, position_ref, first_ref, second_ref, gain_ref, down_ref, up_ref,
                 gains_ref, down_w_ref, up_w_ref, pre_ref, code_ref, flat_ref):
    pre = dot(embed_ref[...], first_ref[...])
    code = dot_exact(pre * lax.logistic(pre), second_ref[...])
    pre_ref[...] = pre
    code_ref[...] = code
    own = pick_row(code, task)
    gain = dot_exact(jnp.broadcast_to(own, (8, own.shape[1])), gain_ref[...])
    for i in range(3):
        gains_ref[i] = 1.0 + gain[:, i * 512 : (i + 1) * 512]
    rows = lax.broadcasted_iota(jnp.int32, (8, own.shape[1]), 0)
    position = position_ref[...].astype(f32)
    codes = own + jnp.where(rows == 0, position[0:1], position[1:2])
    expand, mine, fold = fold_tables()
    flat = dot_exact(codes, down_ref[...])
    for p in range(2):
        for a in range(64):
            flat_ref[a : a + 1, :] = flat[p : p + 1, a * LANES : (a + 1) * LANES]
        spread = jnp.where(mine, dot(expand, flat_ref[...].astype(bf16)), 0.0)
        down_w_ref[p] = dot(spread.astype(bf16), fold).astype(bf16)
    flat = dot_exact(codes, up_ref[...])
    for p in range(2):
        flat_ref[...] = jnp.zeros_like(flat_ref)
        wide = []
        for a in range(RANK):
            wide.append(flat[p : p + 1, a * 512 : (a + 1) * 512])
        wide.append(jnp.zeros((LANES - RANK, 512), f32))
        up_w_ref[p] = jnp.concatenate(wide, axis=0).astype(bf16)


def forward_kernel(
    total_devices, ntask,
    sizes_ref, x_ref, mem_ref, seg_row_ref, seg_col_ref, cot_ref,
    embed_ref, position_ref, first_ref, second_ref, hgain_ref, hdown_ref, hup_ref,
    self_qkv_ref, self_out_ref, cross_qkv_ref, cross_out_ref, ffn_in_ref, ffn_out_ref,
    output_ref, grad_two_ref, ffn_in_grad_ref, ffn_out_grad_ref, up_grad_ref, down_grad_ref, gain_grad_ref,
    gains_ref, down_w_ref, up_w_ref, pre_ref, code_ref,
    in_one_ref, q_ref, k_ref, v_ref, share_one_ref, mixed_one_ref, branch_ref, narrow_ref, after_one_ref,
    in_two_ref, cq_ref, ck_ref, cv_ref, share_two_ref, mixed_two_ref, prob_one_ref, prob_two_ref,
    flat_ref, bias_ref, slot_ref, sem, inner_act_ref, slope_ref, after_two_ref,
):
    row = pl.program_id(0)
    place = lax.axis_index("dp")
    task, size = task_place(sizes_ref, ntask, place)

    @pl.when(row == 0)
    def _():
        hyper_tables(task, embed_ref, position_ref, first_ref, second_ref, hgain_ref, hdown_ref, hup_ref,
                     gains_ref, down_w_ref, up_w_ref, pre_ref, code_ref, flat_ref)

    x = x_ref[0].astype(f32)
    in_one = (x * rms_inv(x) * gains_ref[0, 0:1]).astype(bf16)
    in_one_ref[0] = in_one
    q_ref[0] = (dot(in_one, self_qkv_ref[0]).astype(bf16).astype(f32) * 0.125).astype(bf16)
    k_ref[0] = dot(in_one, self_qkv_ref[1]).astype(bf16)
    v_ref[0] = dot(in_one, self_qkv_ref[2]).astype(bf16)
    memory = mem_ref[0]
    ck_ref[0] = dot(memory, cross_qkv_ref[1]).astype(bf16)
    cv_ref[0] = dot(memory, cross_qkv_ref[2]).astype(bf16)
    queries = lax.broadcasted_iota(jnp.int32, (512, 512), 0)
    keys = lax.broadcasted_iota(jnp.int32, (512, 512), 1)
    allowed = jnp.logical_and(keys <= queries, seg_col_ref[0] == seg_row_ref[0])
    bias_ref[...] = jnp.where(allowed, 0.0, -1e9)

    def attend_row(q_ref, k_ref, v_ref, masked, mixed_ref, share_ref, prob_ref):
        copies = []
        for pair in range(PAIRS):
            lanes = slice(pair * LANES, (pair + 1) * LANES)
            slot = pair % 2
            if pair >= 2:
                copies[pair - 2].wait()
            pair_k = k_ref[0, :, lanes]
            pair_v = v_ref[0, :, lanes]
            ones = jnp.concatenate([pair_v, jnp.ones_like(pair_v)], axis=1)
            for block in range(2):
                rows = slice(block * 256, (block + 1) * 256)
                span = (block + 1) * 256 if masked else 512
                probs, mixed, share = attend_block(
                    q_ref[0, rows, lanes], pair_k[:span], ones[:span],
                    bias_ref[rows, :span] if masked else None,
                )
                for head in range(2):
                    slot_ref[slot, head, rows, :span] = probs[head]
                mixed_ref[0, rows, lanes] = mixed
                share_ref[0, rows, lanes] = share
            copy = pltpu.make_async_copy(
                slot_ref.at[slot], prob_ref.at[row, pl.ds(pair * 2, 2)], sem.at[slot]
            )
            copy.start()
            copies.append(copy)
        copies[PAIRS - 2].wait()
        copies[PAIRS - 1].wait()

    attend_row(q_ref, k_ref, v_ref, True, mixed_one_ref, share_one_ref, prob_one_ref)

    branch = dot(mixed_one_ref[0], self_out_ref[...])
    branch_low = branch.astype(bf16)
    branch_ref[0] = branch_low
    narrow = dot(branch_low, down_w_ref[0])
    narrow_ref[0] = narrow
    narrow_act = (narrow * lax.logistic(narrow)).astype(bf16)
    after_one = x_ref[0].astype(f32) + branch + dot(narrow_act, up_w_ref[0])
    after_one_ref[0] = after_one
    in_two = (after_one * rms_inv(after_one) * gains_ref[1, 0:1]).astype(bf16)
    in_two_ref[0] = in_two
    cq_ref[0] = (dot(in_two, cross_qkv_ref[0]).astype(bf16).astype(f32) * 0.125).astype(bf16)

    attend_row(cq_ref, ck_ref, cv_ref, False, mixed_two_ref, share_two_ref, prob_two_ref)

    after_two = after_one_ref[0] + dot(mixed_two_ref[0], cross_out_ref[...])
    after_two_ref[...] = after_two
    in_three = (after_two * rms_inv(after_two) * gains_ref[2, 0:1]).astype(bf16)
    outer = None
    for c in range(4):
        cols = slice(c * 512, (c + 1) * 512)
        inner = dot(in_three, ffn_in_ref[:, cols])
        phi = 0.5 * (1.0 + lax.erf(inner * 0.7071067811865476))
        slope_ref[:, cols] = phi + inner * jnp.exp2(inner * inner * (-0.5 * LOG2E)) * 0.3989422804014327
        act = (inner * phi).astype(bf16)
        inner_act_ref[:, cols] = act
        part = dot(act, ffn_out_ref[cols, :])
        outer = part if outer is None else outer + part
    outer_low = outer.astype(bf16)
    narrow = dot(outer_low, down_w_ref[1])
    gate = lax.logistic(narrow)
    narrow_act = (narrow * gate).astype(bf16)
    output_ref[0] = (after_two_ref[...] + outer + dot(narrow_act, up_w_ref[1])).astype(bf16)

    keep = jnp.where(row == 0, 0.0, 1.0)
    share = total_devices / (ntask * size.astype(f32))
    grad = cot_ref[0].astype(f32) * share
    grad_low = grad.astype(bf16)
    d_narrow = (dot_nt(grad_low, up_w_ref[1]) * (gate * (1.0 + narrow * (1.0 - gate)))).astype(bf16)
    d_outer = (grad + dot_nt(d_narrow, down_w_ref[1])).astype(bf16)

    @pl.when(row == 0)
    def _():
        up_grad_ref[...] = jnp.zeros_like(up_grad_ref)
        down_grad_ref[...] = jnp.zeros_like(down_grad_ref)
        gain_grad_ref[...] = jnp.zeros_like(gain_grad_ref)
        ffn_in_grad_ref[...] = jnp.zeros_like(ffn_in_grad_ref)
        ffn_out_grad_ref[...] = jnp.zeros_like(ffn_out_grad_ref)

    up_grad_ref[...] += dot_tn(narrow_act, grad_low)[:RANK]
    down_grad_ref[...] += dot_tn(d_narrow, outer_low)[:RANK]
    in_three_t = in_three.T
    d_in = None
    for c in range(4):
        cols = slice(c * 512, (c + 1) * 512)
        ffn_out_grad_ref[cols, :] += dot_tn(inner_act_ref[:, cols], d_outer)
        d_inner = (dot_nt(d_outer, ffn_out_ref[cols, :]) * slope_ref[:, cols]).astype(bf16)
        ffn_in_grad_ref[:, cols] += dot(in_three_t, d_inner)
        part = dot_nt(d_inner, ffn_in_ref[:, cols])
        d_in = part if d_in is None else d_in + part
    after_two = after_two_ref[...]
    d_after, gain_grad = rms_back(after_two, rms_inv(after_two), gains_ref[2, 0:1], d_in)
    grad_two_ref[0] = cot_ref[0].astype(f32) * share + d_after
    gain_grad_ref[...] += jnp.broadcast_to(gain_grad, gain_grad_ref.shape)


def run_forward(tokens, memory, segments, cotangent, group_sizes, params):
    rows, seq, width = tokens.shape
    ff = params[-1].shape[0]
    ntask = group_sizes.shape[0]
    full = lambda *shape: pl.BlockSpec(shape, lambda r: (0,) * len(shape), pipeline_mode=pl.Buffered(1))
    const = lambda *shape: pl.BlockSpec(shape, lambda r: (0,) * len(shape))
    act = pl.BlockSpec((1, seq, width), lambda r: (r, 0, 0))
    nar = pl.BlockSpec((1, seq, LANES), lambda r: (r, 0, 0))
    out = lambda shape, dtype: jax.ShapeDtypeStruct(shape, dtype)
    wide = (rows, seq, width)
    any_spec = pl.BlockSpec(memory_space=pl.ANY)
    heads = 2 * PAIRS
    outs = [
        (act, out(wide, bf16)), (act, out(wide, f32)),
        (const(width, ff), out((width, ff), f32)), (const(ff, width), out((ff, width), f32)),
        (const(RANK, width), out((RANK, width), f32)), (const(RANK, width), out((RANK, width), f32)),
        (const(8, width), out((8, width), f32)),
        (const(3, 8, width), out((3, 8, width), f32)),
        (const(2, width, LANES), out((2, width, LANES), bf16)), (const(2, LANES, width), out((2, LANES, width), bf16)),
        (const(ntask, params[2].shape[1]), out((ntask, params[2].shape[1]), f32)),
        (const(ntask, params[0].shape[1]), out((ntask, params[0].shape[1]), f32)),
        (act, out(wide, bf16)), (act, out(wide, bf16)), (act, out(wide, bf16)), (act, out(wide, bf16)),
        (act, out(wide, f32)), (act, out(wide, bf16)), (act, out(wide, bf16)), (nar, out((rows, seq, LANES), f32)),
        (act, out(wide, f32)),
        (act, out(wide, bf16)), (act, out(wide, bf16)), (act, out(wide, bf16)), (act, out(wide, bf16)),
        (act, out(wide, f32)), (act, out(wide, bf16)),
        (any_spec, out((rows, heads, seq, seq), bf16)), (any_spec, out((rows, heads, seq, seq), bf16)),
    ]
    return pl.pallas_call(
        functools.partial(forward_kernel, lax.axis_size("dp"), ntask),
        grid=(rows,),
        in_specs=[
            pl.BlockSpec(memory_space=pltpu.SMEM), act, act,
            pl.BlockSpec((1, 1, seq), lambda r: (r, 0, 0)), pl.BlockSpec((1, seq, 1), lambda r: (r, 0, 0)), act,
        ] + [full(*item.shape) for item in params],
        out_specs=[spec for spec, _ in outs],
        out_shape=[shape for _, shape in outs],
        scratch_shapes=[
            pltpu.VMEM((64, LANES), f32), pltpu.VMEM((seq, seq), f32), pltpu.VMEM((2, 2, seq, seq), bf16),
            pltpu.SemaphoreType.DMA((2,)), pltpu.VMEM((seq, ff), bf16), pltpu.VMEM((seq, ff), f32),
            pltpu.VMEM((seq, width), f32),
        ],
        compiler_params=pltpu.CompilerParams(vmem_limit_bytes=60 << 20),
    )(group_sizes, tokens, memory, segments[:, None, :], segments[:, :, None], cotangent, *params)


def attend_back(q_ref, k_ref, v_ref, mixed_ref, share_ref, prob_ref, d_mixed_ref, masked, dq_ref, dk_ref, dv_ref):
    low = low_lanes()
    for pair in range(PAIRS):
        lanes = slice(pair * LANES, (pair + 1) * LANES)
        grad = d_mixed_ref[:, lanes].astype(f32) * share_ref[0, :, lanes]
        product = grad * mixed_ref[0, :, lanes].astype(f32)
        grad = grad.astype(bf16)
        q, k, v = q_ref[0, :, lanes], k_ref[0, :, lanes], v_ref[0, :, lanes]
        zero = jnp.zeros_like(q)
        dq = [None, None]
        whole = [None, None]
        half = [None, None]
        add = lambda old, new: new if old is None else old + new
        for head in range(2):
            own = low if head == 0 else jnp.logical_not(low)
            delta = jnp.sum(jnp.where(own, product, 0.0), axis=-1, keepdims=True)
            head_g, head_q, head_k = (jnp.where(own, item, zero) for item in (grad, q, k))
            for block in range(2):
                rows = slice(block * 256, (block + 1) * 256)
                span = (block + 1) * 256 if masked else 512
                prob = prob_ref[0, pair * 2 + head, rows, :span]
                d_prob = dot_nt(head_g[rows], v[:span])
                d_score = (prob.astype(f32) * (d_prob - delta[rows])).astype(bf16)
                dq[block] = add(dq[block], dot(d_score, head_k[:span]))
                kind = half if span == 256 else whole
                kind[0] = add(kind[0], dot_tn(head_q[rows], d_score))
                kind[1] = add(kind[1], dot_tn(head_g[rows], prob))
        for block in range(2):
            dq_ref[block * 256 : (block + 1) * 256, lanes] = (dq[block] * 0.125).astype(bf16)
        for out_ref, both, first in ((dk_ref, whole[0], half[0]), (dv_ref, whole[1], half[1])):
            if first is None:
                out_ref[:, lanes] = both.T.astype(bf16)
            else:
                out_ref[:256, lanes] = (both[:, :256] + first).T.astype(bf16)
                out_ref[256:, lanes] = both[:, 256:].T.astype(bf16)


def cross_back_kernel(
    grad_two_ref, mixed_ref, q_ref, k_ref, v_ref, share_ref, prob_ref, mem_ref, in_two_ref, after_one_ref,
    narrow_ref, branch_ref, gains_ref, down_w_ref, up_w_ref, cross_qkv_ref, cross_out_ref,
    out_grad_ref, qkv_grad_ref, mem_grad_ref, grad_one_ref, d_branch_ref, up_grad_ref, down_grad_ref, gain_grad_ref,
    d_mixed_ref, dq_ref, dk_ref, dv_ref,
):
    row = pl.program_id(0)

    @pl.when(row == 0)
    def _():
        for ref in (out_grad_ref, qkv_grad_ref, up_grad_ref, down_grad_ref, gain_grad_ref):
            ref[...] = jnp.zeros_like(ref)

    grad_low = grad_two_ref[0].astype(bf16)
    out_grad_ref[...] += dot_tn(mixed_ref[0], grad_low)
    d_mixed_ref[...] = dot_nt(grad_low, cross_out_ref[...]).astype(bf16)
    attend_back(q_ref, k_ref, v_ref, mixed_ref, share_ref, prob_ref, d_mixed_ref, False, dq_ref, dk_ref, dv_ref)
    qkv_grad_ref[0] += dot_tn(in_two_ref[0], dq_ref[...])
    memory_t = mem_ref[0].T
    qkv_grad_ref[1] += dot(memory_t, dk_ref[...])
    qkv_grad_ref[2] += dot(memory_t, dv_ref[...])
    mem_grad_ref[0] = dot_nt(dk_ref[...], cross_qkv_ref[1]) + dot_nt(dv_ref[...], cross_qkv_ref[2])
    d_in = dot_nt(dq_ref[...], cross_qkv_ref[0])
    after_one = after_one_ref[0]
    d_after, gain_grad = rms_back(after_one, rms_inv(after_one), gains_ref[1, 0:1], d_in)
    gain_grad_ref[...] += jnp.broadcast_to(gain_grad, gain_grad_ref.shape)
    grad = grad_two_ref[0] + d_after
    grad_one_ref[0] = grad
    grad_low = grad.astype(bf16)
    narrow = narrow_ref[0]
    gate = lax.logistic(narrow)
    narrow_act = (narrow * gate).astype(bf16)
    up_grad_ref[...] += dot_tn(narrow_act, grad_low)[:RANK]
    d_narrow = (dot_nt(grad_low, up_w_ref[0]) * (gate * (1.0 + narrow * (1.0 - gate)))).astype(bf16)
    down_grad_ref[...] += dot_tn(d_narrow, branch_ref[0])[:RANK]
    d_branch_ref[0] = (grad + dot_nt(d_narrow, down_w_ref[0])).astype(bf16)


def self_back_kernel(
    d_branch_ref, mixed_ref, q_ref, k_ref, v_ref, share_ref, prob_ref, in_one_ref, x_ref, grad_one_ref, gains_ref,
    self_qkv_ref, self_out_ref,
    out_grad_ref, qkv_grad_ref, input_grad_ref, gain_grad_ref,
    d_mixed_ref, dq_ref, dk_ref, dv_ref,
):
    row = pl.program_id(0)

    @pl.when(row == 0)
    def _():
        for ref in (out_grad_ref, qkv_grad_ref, gain_grad_ref):
            ref[...] = jnp.zeros_like(ref)

    out_grad_ref[...] += dot_tn(mixed_ref[0], d_branch_ref[0])
    d_mixed_ref[...] = dot_nt(d_branch_ref[0], self_out_ref[...]).astype(bf16)
    attend_back(q_ref, k_ref, v_ref, mixed_ref, share_ref, prob_ref, d_mixed_ref, True, dq_ref, dk_ref, dv_ref)
    in_one_t = in_one_ref[0].T
    d_in = None
    for j, ref in enumerate((dq_ref, dk_ref, dv_ref)):
        qkv_grad_ref[j] += dot(in_one_t, ref[...])
        part = dot_nt(ref[...], self_qkv_ref[j])
        d_in = part if d_in is None else d_in + part
    x = x_ref[0].astype(f32)
    d_x, gain_grad = rms_back(x, rms_inv(x), gains_ref[0, 0:1], d_in)
    gain_grad_ref[...] += jnp.broadcast_to(gain_grad, gain_grad_ref.shape)
    input_grad_ref[0] = grad_one_ref[0] + d_x


def small_kernel(
    ntask, sizes_ref, up_one_ref, up_two_ref, down_one_ref, down_two_ref, gain_one_ref, gain_two_ref, gain_three_ref,
    embed_ref, first_ref, second_ref, hgain_ref, hdown_ref, hup_ref, pre_ref,
    out_ref, flat_ref, fold_ref,
):
    task, _ = task_place(sizes_ref, ntask, lax.axis_index("dp"))
    _, mine, fold = fold_tables()
    unfold = fold.astype(f32)
    pair_row = lax.broadcasted_iota(jnp.int32, (2 * ntask, LANES), 0)
    task_row = lax.broadcasted_iota(jnp.int32, (ntask, LANES), 0)
    for p, ref in enumerate((down_one_ref, down_two_ref)):
        tall = jnp.concatenate([ref[...], jnp.zeros((LANES - RANK, ref.shape[1]), f32)], axis=0).T
        spread = lax.dot_general(tall, unfold, (((1,), (1,)), ((), ())), precision=highest, preferred_element_type=f32)
        spread = jnp.where(mine, spread, 0.0)
        fold_ref[p] = jnp.sum(spread.reshape(64, 8, LANES), axis=1)
        for a in range(64):
            flat_ref[p : p + 1, a * LANES : (a + 1) * LANES] = fold_ref[p, a : a + 1]
        for a in range(RANK):
            flat_ref[2 + p : 3 + p, a * 512 : (a + 1) * 512] = (up_one_ref, up_two_ref)[p][a : a + 1, :]
    flat_ref[4:8, :] = jnp.zeros((4, flat_ref.shape[1]), f32)
    for a in range(64):
        lanes = slice((a % 4) * LANES, (a % 4 + 1) * LANES)
        r = a // 4
        for base, first_row, second_row in (
            (0, fold_ref[0, a : a + 1], fold_ref[1, a : a + 1]),
            (1024, up_one_ref[r : r + 1, lanes], up_two_ref[r : r + 1, lanes]),
        ):
            block = jnp.where(pair_row == 2 * task, first_row, jnp.where(pair_row == 2 * task + 1, second_row, 0.0))
            out_ref[base + a * 16 : base + (a + 1) * 16, :] = block
    gain = []
    for ref in (gain_one_ref, gain_two_ref, gain_three_ref):
        gain.append(ref[...])
    gain = jnp.concatenate(gain, axis=1)
    for j in range(12):
        block = jnp.where(task_row == task, gain[:, j * LANES : (j + 1) * LANES], 0.0)
        out_ref[2048 + j * 8 : 2056 + j * 8, :] = block
    flat = flat_ref[...]
    down_code = dot_exact_nt(flat, hdown_ref[...])
    up_code = dot_exact_nt(flat, hup_ref[...])
    d_codes = down_code[0:2] + up_code[2:4]
    d_code = d_codes[0:1] + d_codes[1:2] + dot_exact_nt(gain, hgain_ref[...])[0:1]
    one_row = lax.broadcasted_iota(jnp.int32, (8, 1), 0) == 0
    d_code = jnp.where(one_row, jnp.broadcast_to(d_code, (8, d_code.shape[1])), 0.0)
    pre = pick_row(pre_ref[...], task)
    embed = pick_row(embed_ref[...].astype(f32), task)
    hidden = jnp.broadcast_to(pre * lax.logistic(pre), (8, pre.shape[1]))
    exact_tn = lambda left, right: lax.dot_general(
        left, right, (((0,), (0,)), ((), ())), precision=highest, preferred_element_type=f32
    )
    own_second = exact_tn(hidden, d_code)
    d_pre = silu_back(pre, dot_exact_nt(d_code, second_ref[...]))
    own_first = exact_tn(jnp.broadcast_to(embed, (8, embed.shape[1])), d_pre)
    own_task = dot_exact_nt(d_pre, first_ref[...])[0:1]
    rows = lax.broadcasted_iota(jnp.int32, (8, own_task.shape[1]), 0)
    task_block = jnp.where(rows == task, own_task, 0.0)
    code_block = jnp.where(rows == 0, d_codes[0:1], jnp.where(rows == 1, d_codes[1:2], 0.0))
    out_ref[2144:2208, :] = own_first
    out_ref[2208:2336, :] = jnp.concatenate([own_second, jnp.zeros_like(own_second)], axis=1)
    out_ref[2336:2344, :] = jnp.concatenate([task_block, code_block], axis=1)
    out_ref[2344:, :] = jnp.zeros((out_ref.shape[0] - 2344, LANES), f32)


def spread_kernel(
    ntask, sum_ref, code_ref, position_ref,
    task_ref, pos_ref, first_ref, second_ref, gain_ref, down_ref, up_ref,
):
    code = code_ref[...]
    emb = code.shape[1]
    position = position_ref[...].astype(f32)
    codes = jnp.stack([code + position[0:1], code + position[1:2]], axis=1).reshape(2 * ntask, emb)
    exact_tn = lambda left, right: lax.dot_general(
        left, right, (((0,), (0,)), ((), ())), precision=highest, preferred_element_type=f32
    )
    wide = lambda base, count, step: jnp.concatenate(
        [sum_ref[base + a * step : base + (a + 1) * step, :] for a in range(count)], axis=1
    )
    down_ref[...] = exact_tn(codes, wide(0, 64, 16))
    up_ref[...] = exact_tn(codes, wide(1024, 64, 16))
    gain_ref[...] = exact_tn(code, wide(2048, 12, 8))
    first_ref[...] = sum_ref[2144:2208, :]
    second_ref[...] = sum_ref[2208:2336, :emb]
    task_ref[...] = sum_ref[2336:2344, :emb]
    pos_ref[...] = sum_ref[2336:2338, emb:]


def call_rows(kernel, rows, ins, outs, scratch, limit=60):
    def spec(item, blocked):
        shape = item.shape
        if blocked:
            return pl.BlockSpec((1,) + tuple(shape[1:]), lambda r: (r,) + (0,) * (len(shape) - 1))
        return pl.BlockSpec(tuple(shape), lambda r: (0,) * len(shape))

    return pl.pallas_call(
        kernel,
        grid=(rows,),
        in_specs=[spec(*item) for item in ins],
        out_specs=[spec(*item) for item in outs],
        out_shape=[item for item, _ in outs],
        scratch_shapes=scratch,
        compiler_params=pltpu.CompilerParams(vmem_limit_bytes=limit << 20),
    )(*[item for item, _ in ins])


ORDER_A = ((1, 1), (2, 4), (4, 2), (8, 8), (16, 16))
ORDER_B = ((1, 1), (2, 4), (8, 8), (16, 16), (4, 2))


def all_sum(total, order):
    devices = lax.axis_size("dp")
    place = lax.axis_index("dp")

    def swap(values, even_bit, odd_bit):
        moves = [(i, i ^ (odd_bit if i % 2 else even_bit)) for i in range(devices)]
        return lax.ppermute(values, "dp", moves)

    def upper(even_bit, odd_bit):
        return jnp.where(place % 2 == 1, (place // odd_bit) % 2, (place // even_bit) % 2)

    for even_bit, odd_bit in order:
        half = total.shape[0] // 2
        side = upper(even_bit, odd_bit)
        sent = lax.dynamic_slice_in_dim(total, (1 - side) * half, half)
        kept = lax.dynamic_slice_in_dim(total, side * half, half)
        total = kept + swap(sent, even_bit, odd_bit)
    high = 32
    while high < devices:
        total = total + swap(total, high, high)
        high *= 2
    for even_bit, odd_bit in order[::-1]:
        side = upper(even_bit, odd_bit)
        other = swap(total, even_bit, odd_bit)
        total = jnp.concatenate(
            [jnp.where(side == 0, total, other), jnp.where(side == 0, other, total)]
        )
    return total


def on_device(
    tokens, memory, segments, cotangent, group_sizes, task_embed, position_embed, hyper_first, hyper_second,
    hyper_gain, hyper_down, hyper_up, self_qkv, self_out, cross_qkv, cross_out, ffn_in, ffn_out,
):
    rows, seq, width = tokens.shape
    ntask = group_sizes.shape[0]
    params = (
        task_embed, position_embed, hyper_first, hyper_second, hyper_gain, hyper_down, hyper_up,
        self_qkv, self_out, cross_qkv, cross_out, ffn_in, ffn_out,
    )
    (
        output, grad_two, ffn_in_grad, ffn_out_grad, up_two, down_two, gain_three,
        gains, down_w, up_w, pre, code,
        in_one, q_one, k_one, v_one, share_one, mixed_one, branch, narrow, after_one,
        in_two, q_two, k_two, v_two, share_two, mixed_two, prob_one, prob_two,
    ) = run_forward(tokens, memory, segments, cotangent, group_sizes, params)
    like = lambda shape, dtype=f32: jax.ShapeDtypeStruct(shape, dtype)
    wide = tokens.shape
    row_scratch = [pltpu.VMEM((seq, width), bf16)] * 4
    cross_out_grad, cross_qkv_grad, memory_grad, grad_one, d_branch, up_one, down_one, gain_two = call_rows(
        cross_back_kernel,
        rows,
        [
            (grad_two, True), (mixed_two, True), (q_two, True), (k_two, True), (v_two, True), (share_two, True),
            (prob_two, True), (memory, True), (in_two, True), (after_one, True), (narrow, True), (branch, True),
            (gains, False), (down_w, False), (up_w, False), (cross_qkv, False), (cross_out, False),
        ],
        [
            (like(cross_out.shape), False), (like(cross_qkv.shape), False), (like(wide), True), (like(wide), True),
            (like(wide, bf16), True), (like((RANK, width)), False), (like((RANK, width)), False), (like((8, width)), False),
        ],
        row_scratch,
    )
    self_out_grad, self_qkv_grad, input_grad, gain_one = call_rows(
        self_back_kernel,
        rows,
        [
            (d_branch, True), (mixed_one, True), (q_one, True), (k_one, True), (v_one, True), (share_one, True),
            (prob_one, True), (in_one, True), (tokens, True), (grad_one, True), (gains, False),
            (self_qkv, False), (self_out, False),
        ],
        [(like(self_out.shape), False), (like(self_qkv.shape), False), (like(wide), True), (like((8, width)), False)],
        row_scratch,
    )
    small = pl.pallas_call(
        functools.partial(small_kernel, ntask),
        out_shape=like((2560, LANES)),
        in_specs=[pl.BlockSpec(memory_space=pltpu.SMEM)] + [pl.BlockSpec(memory_space=pltpu.VMEM)] * 14,
        out_specs=pl.BlockSpec(memory_space=pltpu.VMEM),
        scratch_shapes=[pltpu.VMEM((8, 8192), f32), pltpu.VMEM((2, 64, LANES), f32)],
        compiler_params=pltpu.CompilerParams(vmem_limit_bytes=32 << 20),
    )(
        group_sizes, up_one, up_two, down_one, down_two, gain_one, gain_two, gain_three,
        task_embed, hyper_first, hyper_second, hyper_gain, hyper_down, hyper_up, pre,
    )
    sum_out = all_sum(ffn_out_grad, ORDER_A)
    sum_in = all_sum(ffn_in_grad, ORDER_B)
    cross_rows = jnp.concatenate([cross_out_grad[None], cross_qkv_grad]).reshape(-1, width)
    sum_cross = all_sum(cross_rows, ORDER_A).reshape(4, width, width)
    self_rows = jnp.concatenate([self_out_grad[None], self_qkv_grad]).reshape(-1, width)
    sum_self = all_sum(self_rows, ORDER_B).reshape(4, width, width)
    sum_small = all_sum(small, ORDER_A)
    task_grad, position_grad, first_grad, second_grad, gain_grad, down_grad, up_grad = pl.pallas_call(
        functools.partial(spread_kernel, ntask),
        out_shape=[
            like(item.shape)
            for item in (task_embed, position_embed, hyper_first, hyper_second, hyper_gain, hyper_down, hyper_up)
        ],
        compiler_params=pltpu.CompilerParams(vmem_limit_bytes=32 << 20),
    )(sum_small, code, position_embed)
    return (
        output, input_grad, memory_grad, task_grad, position_grad, first_grad, second_grad, gain_grad, down_grad,
        up_grad, sum_self[1:], sum_self[0], sum_cross[1:], sum_cross[0], sum_in, sum_out,
    )


def solution(mesh):
    split = P("dp", None, None)
    return jax.shard_map(
        on_device,
        mesh=mesh,
        in_specs=(split, split, P("dp", None), split) + (P(),) * 14,
        out_specs=(split,) * 3 + (P(),) * 13,
        check_vma=False,
    )
```

```python
import functools

import jax
import jax.numpy as jnp
from jax import lax
from jax.experimental import pallas as pl
from jax.experimental.pallas import tpu as pltpu
from jax.sharding import PartitionSpec as P

PAIRS = 4
LANES = 128
RANK = 16
LOG2E = 1.4426950408889634
epsilon = 1e-06
highest = lax.Precision.HIGHEST
f32 = jnp.float32
bf16 = jnp.bfloat16
SHORT = pl.CostEstimate(flops=1, bytes_accessed=1, transcendentals=0)


def dot(left, right):
    return jnp.dot(left, right, preferred_element_type=f32)


def dot_nt(left, right):
    return lax.dot_general(left, right, (((1,), (1,)), ((), ())), preferred_element_type=f32)


def dot_tn(left, right):
    return lax.dot_general(left, right, (((0,), (0,)), ((), ())), preferred_element_type=f32)


def three(values):
    high = values.astype(bf16)
    rest = values - high.astype(f32)
    mid = rest.astype(bf16)
    return high, mid, (rest - mid.astype(f32)).astype(bf16)


def dot_exact(values, table):
    high, mid, low = three(values)
    return dot(high, table) + (dot(mid, table) + dot(low, table))


def dot_exact_nt(values, table):
    high, mid, low = three(values)
    return dot_nt(high, table) + (dot_nt(mid, table) + dot_nt(low, table))


def rms_back(values, inv, gain, grad):
    unit = values * inv
    scaled = grad * gain
    mean = jnp.mean(scaled * unit, axis=-1, keepdims=True)
    return inv * (scaled - unit * mean), jnp.sum(grad * unit, axis=0, keepdims=True)


def rms_inv(values):
    return lax.rsqrt(jnp.mean(values * values, axis=-1, keepdims=True) + epsilon)


def low_lanes():
    return lax.broadcasted_iota(jnp.int32, (1, LANES), 1) < 64


def silu_back(values, grad):
    gate = lax.logistic(values)
    return grad * (gate * (1.0 + values * (1.0 - gate)))


def task_place(sizes_ref, count, place):
    end, task = jnp.int32(0), jnp.int32(0)
    for i in range(count):
        end = end + sizes_ref[i]
        task = task + jnp.where(end <= place, 1, 0)
    size = sizes_ref[0]
    for i in range(1, count):
        size = jnp.where(task == i, sizes_ref[i], size)
    return task, size


def pick_row(table, task):
    rows = lax.broadcasted_iota(jnp.int32, table.shape, 0)
    return jnp.sum(jnp.where(rows == task, table, 0.0), axis=0, keepdims=True)


def fold_tables():
    feature = lax.broadcasted_iota(jnp.int32, (512, 64), 0)
    block = lax.broadcasted_iota(jnp.int32, (512, 64), 1)
    expand = jnp.where(feature // 8 == block, 1.0, 0.0).astype(bf16)
    feature = lax.broadcasted_iota(jnp.int32, (512, LANES), 0)
    lane = lax.broadcasted_iota(jnp.int32, (512, LANES), 1)
    own = (lane // RANK) == (feature % 8)
    row = lax.broadcasted_iota(jnp.int32, (LANES, LANES), 0)
    lane = lax.broadcasted_iota(jnp.int32, (LANES, LANES), 1)
    fold = jnp.where((row % RANK) == lane, 1.0, 0.0).astype(bf16)
    return expand, own, fold


def upper(place, bits):
    return lax.rem(jnp.where(lax.rem(place, 2) == 1, place // bits[1], place // bits[0]), 2)


def halves(total_ref, kept_ref, sent_ref, sem, base):
    half = total_ref.shape[0] // 2
    side = lax.rem(lax.axis_index("dp"), 2)
    return (
        pltpu.make_async_copy(total_ref.at[pl.ds(pl.multiple_of((1 - side) * half, half), half)], sent_ref, sem.at[base]),
        pltpu.make_async_copy(total_ref.at[pl.ds(pl.multiple_of(side * half, half), half)], kept_ref, sem.at[base + 1]),
    )


def attend_block(pair_q, keys, values_ones, bias):
    low = low_lanes()
    probs, mixed = [], []
    for head in range(2):
        own = low if head == 0 else jnp.logical_not(low)
        scores = dot_nt(jnp.where(own, pair_q, jnp.zeros_like(pair_q)), keys)
        if bias is not None:
            scores = scores + bias
        top = jnp.max(scores, axis=-1, keepdims=True)
        prob = jnp.exp2((scores - top) * LOG2E).astype(bf16)
        probs.append(prob)
        mixed.append(dot(prob, values_ones))
    total = jnp.where(low, mixed[0][:, LANES:], mixed[1][:, LANES:])
    share = 1.0 / total
    out = jnp.where(low, mixed[0][:, :LANES], mixed[1][:, :LANES]) * share
    return probs, out.astype(bf16), share


def hyper_tables(task, embed_ref, position_ref, first_ref, second_ref, gain_ref, down_ref, up_ref,
                 gains_ref, down_w_ref, up_w_ref, pre_ref, code_ref, flat_ref):
    pre = dot(embed_ref[...], first_ref[...])
    code = dot_exact_nt(pre * lax.logistic(pre), second_ref[...])
    pre_ref[...] = pre
    code_ref[...] = code
    own = pick_row(code, task)
    gain = dot_exact(jnp.broadcast_to(own, (8, own.shape[1])), gain_ref[...])
    for i in range(3):
        gains_ref[i] = 1.0 + gain[:, i * 512 : (i + 1) * 512]
    rows = lax.broadcasted_iota(jnp.int32, (8, own.shape[1]), 0)
    position = position_ref[...].astype(f32)
    codes = own + jnp.where(rows == 0, position[0:1], position[1:2])
    expand, mine, fold = fold_tables()
    flat = dot_exact(codes, down_ref[...])
    for p in range(2):
        for a in range(64):
            flat_ref[a : a + 1, :] = flat[p : p + 1, a * LANES : (a + 1) * LANES]
        spread = jnp.where(mine, dot(expand, flat_ref[...].astype(bf16)), 0.0)
        down_w_ref[p] = dot(spread.astype(bf16), fold).astype(bf16)
    flat = dot_exact(codes, up_ref[...])
    for p in range(2):
        flat_ref[...] = jnp.zeros_like(flat_ref)
        wide = []
        for a in range(RANK):
            wide.append(flat[p : p + 1, a * 512 : (a + 1) * 512])
        wide.append(jnp.zeros((LANES - RANK, 512), f32))
        up_w_ref[p] = jnp.concatenate(wide, axis=0).astype(bf16)


def forward_kernel(
    total_devices, ntask,
    sizes_ref, x_ref, mem_ref, seg_ref, cot_ref,
    embed_ref, position_ref, first_ref, second_ref, hgain_ref, hdown_ref, hup_ref,
    self_qkv_ref, self_out_ref, cross_qkv_ref, cross_out_ref, ffn_in_ref, ffn_out_ref,
    output_ref, grad_two_ref, in_kept_ref, in_sent_ref, out_kept_ref, out_sent_ref, up_grad_ref, down_grad_ref, gain_grad_ref,
    gains_ref, down_w_ref, up_w_ref, pre_ref, code_ref,
    in_one_ref, q_ref, k_ref, v_ref, share_one_ref, mixed_one_ref, branch_ref, narrow_ref, after_one_ref,
    in_two_ref, cq_ref, ck_ref, cv_ref, share_two_ref, mixed_two_ref, prob_one_ref, prob_two_ref,
    flat_ref, bias_ref, slot_ref, sem, inner_act_ref, slope_ref, after_two_ref,
    ffn_in_grad_ref, ffn_out_grad_ref, part_sem,
):
    row = pl.program_id(0)
    place = lax.axis_index("dp")
    task, size = task_place(sizes_ref, ntask, place)

    @pl.when(row == 0)
    def _():
        hyper_tables(task, embed_ref, position_ref, first_ref, second_ref, hgain_ref, hdown_ref, hup_ref,
                     gains_ref, down_w_ref, up_w_ref, pre_ref, code_ref, flat_ref)

    x = x_ref[0].astype(f32)
    in_one = (x * rms_inv(x) * gains_ref[0, 0:1]).astype(bf16)
    in_one_ref[0] = in_one
    q_ref[0] = (dot(in_one, self_qkv_ref[0]).astype(bf16).astype(f32) * 0.125).astype(bf16)
    k_ref[0] = dot(in_one, self_qkv_ref[1]).astype(bf16)
    v_ref[0] = dot(in_one, self_qkv_ref[2]).astype(bf16)
    memory = mem_ref[0]
    ck_ref[0] = dot(memory, cross_qkv_ref[1]).astype(bf16)
    cv_ref[0] = dot(memory, cross_qkv_ref[2]).astype(bf16)
    queries = lax.broadcasted_iota(jnp.int32, (512, 512), 0)
    keys = lax.broadcasted_iota(jnp.int32, (512, 512), 1)
    segment = seg_ref[pl.ds(row, 1), :].astype(f32)
    segment_q = jnp.broadcast_to(segment, (LANES, segment.shape[1])).T[:, 0:1]
    allowed = jnp.logical_and(keys <= queries, segment_q == segment)
    bias_ref[...] = jnp.where(allowed, 0.0, -1e9)

    def attend_row(q_ref, k_ref, v_ref, masked, mixed_ref, share_ref, prob_ref):
        copies = []
        for pair in range(PAIRS):
            lanes = slice(pair * LANES, (pair + 1) * LANES)
            slot = pair % 2
            if pair >= 2:
                copies[pair - 2].wait()
            pair_k = k_ref[0, :, lanes]
            pair_v = v_ref[0, :, lanes]
            ones = jnp.concatenate([pair_v, jnp.ones_like(pair_v)], axis=1)
            for block in range(2):
                rows = slice(block * 256, (block + 1) * 256)
                span = (block + 1) * 256 if masked else 512
                probs, mixed, share = attend_block(
                    q_ref[0, rows, lanes], pair_k[:span], ones[:span],
                    bias_ref[rows, :span] if masked else None,
                )
                for head in range(2):
                    slot_ref[slot, head, rows, :span] = probs[head]
                mixed_ref[0, rows, lanes] = mixed
                share_ref[0, rows, lanes] = share
            copy = pltpu.make_async_copy(
                slot_ref.at[slot], prob_ref.at[row, pl.ds(pair * 2, 2)], sem.at[slot]
            )
            copy.start()
            copies.append(copy)
        copies[PAIRS - 2].wait()
        copies[PAIRS - 1].wait()

    attend_row(q_ref, k_ref, v_ref, True, mixed_one_ref, share_one_ref, prob_one_ref)

    branch = dot(mixed_one_ref[0], self_out_ref[...])
    branch_low = branch.astype(bf16)
    branch_ref[0] = branch_low
    narrow = dot(branch_low, down_w_ref[0])
    narrow_ref[0] = narrow
    narrow_act = (narrow * lax.logistic(narrow)).astype(bf16)
    after_one = x_ref[0].astype(f32) + branch + dot(narrow_act, up_w_ref[0])
    after_one_ref[0] = after_one
    in_two = (after_one * rms_inv(after_one) * gains_ref[1, 0:1]).astype(bf16)
    in_two_ref[0] = in_two
    cq_ref[0] = (dot(in_two, cross_qkv_ref[0]).astype(bf16).astype(f32) * 0.125).astype(bf16)

    attend_row(cq_ref, ck_ref, cv_ref, False, mixed_two_ref, share_two_ref, prob_two_ref)

    after_two = after_one_ref[0] + dot(mixed_two_ref[0], cross_out_ref[...])
    after_two_ref[...] = after_two
    in_three = (after_two * rms_inv(after_two) * gains_ref[2, 0:1]).astype(bf16)
    outer = None
    for c in range(4):
        cols = slice(c * 512, (c + 1) * 512)
        inner = dot(in_three, ffn_in_ref[:, cols])
        phi = 0.5 * (1.0 + lax.erf(inner * 0.7071067811865476))
        slope_ref[:, cols] = phi + inner * jnp.exp2(inner * inner * (-0.5 * LOG2E)) * 0.3989422804014327
        act = (inner * phi).astype(bf16)
        inner_act_ref[:, cols] = act
        part = dot(act, ffn_out_ref[cols, :])
        outer = part if outer is None else outer + part
    outer_low = outer.astype(bf16)
    narrow = dot(outer_low, down_w_ref[1])
    gate = lax.logistic(narrow)
    narrow_act = (narrow * gate).astype(bf16)
    output_ref[0] = (after_two_ref[...] + outer + dot(narrow_act, up_w_ref[1])).astype(bf16)

    keep = jnp.where(row == 0, 0.0, 1.0)
    share = total_devices / (ntask * size.astype(f32))
    grad = cot_ref[0].astype(f32) * share
    grad_low = grad.astype(bf16)
    d_narrow = (dot_nt(grad_low, up_w_ref[1]) * (gate * (1.0 + narrow * (1.0 - gate)))).astype(bf16)
    d_outer = (grad + dot_nt(d_narrow, down_w_ref[1])).astype(bf16)

    @pl.when(row == 0)
    def _():
        up_grad_ref[...] = jnp.zeros_like(up_grad_ref)
        down_grad_ref[...] = jnp.zeros_like(down_grad_ref)
        gain_grad_ref[...] = jnp.zeros_like(gain_grad_ref)
        ffn_in_grad_ref[...] = jnp.zeros_like(ffn_in_grad_ref)
        ffn_out_grad_ref[...] = jnp.zeros_like(ffn_out_grad_ref)

    up_grad_ref[...] += dot_tn(narrow_act, grad_low)[:RANK]
    down_grad_ref[...] += dot_tn(d_narrow, outer_low)[:RANK]
    for c in range(4):
        cols = slice(c * 512, (c + 1) * 512)
        ffn_out_grad_ref[cols, :] += dot_tn(inner_act_ref[:, cols], d_outer)

    last = row == pl.num_programs(0) - 1

    @pl.when(last)
    def _():
        for copy in halves(ffn_out_grad_ref, out_kept_ref, out_sent_ref, part_sem, 0):
            copy.start()

    in_three_t = in_three.T
    d_in = None
    for c in range(4):
        cols = slice(c * 512, (c + 1) * 512)
        d_inner = (dot_nt(d_outer, ffn_out_ref[cols, :]) * slope_ref[:, cols]).astype(bf16)
        ffn_in_grad_ref[:, cols] += dot(in_three_t, d_inner)
        part = dot_nt(d_inner, ffn_in_ref[:, cols])
        d_in = part if d_in is None else d_in + part

    @pl.when(last)
    def _():
        for copy in halves(ffn_in_grad_ref, in_kept_ref, in_sent_ref, part_sem, 2):
            copy.start()

    after_two = after_two_ref[...]
    d_after, gain_grad = rms_back(after_two, rms_inv(after_two), gains_ref[2, 0:1], d_in)
    grad_two_ref[0] = cot_ref[0].astype(f32) * share + d_after
    gain_grad_ref[...] += jnp.broadcast_to(gain_grad, gain_grad_ref.shape)

    @pl.when(last)
    def _():
        for copy in halves(ffn_out_grad_ref, out_kept_ref, out_sent_ref, part_sem, 0):
            copy.wait()
        for copy in halves(ffn_in_grad_ref, in_kept_ref, in_sent_ref, part_sem, 2):
            copy.wait()


def run_forward(tokens, memory, segments, cotangent, group_sizes, params):
    rows, seq, width = tokens.shape
    ff = params[-1].shape[0]
    ntask = group_sizes.shape[0]
    full = lambda *shape: pl.BlockSpec(shape, lambda r: (0,) * len(shape), pipeline_mode=pl.Buffered(1))
    const = lambda *shape: pl.BlockSpec(shape, lambda r: (0,) * len(shape))
    act = pl.BlockSpec((1, seq, width), lambda r: (r, 0, 0))
    nar = pl.BlockSpec((1, seq, LANES), lambda r: (r, 0, 0))
    out = lambda shape, dtype: jax.ShapeDtypeStruct(shape, dtype)
    wide = (rows, seq, width)
    any_spec = pl.BlockSpec(memory_space=pl.ANY)
    heads = 2 * PAIRS
    outs = [
        (act, out(wide, bf16)), (act, out(wide, f32)),
        (any_spec, out((width // 2, ff), f32)), (any_spec, out((width // 2, ff), f32)),
        (any_spec, out((ff // 2, width), f32)), (any_spec, out((ff // 2, width), f32)),
        (const(RANK, width), out((RANK, width), f32)), (const(RANK, width), out((RANK, width), f32)),
        (const(8, width), out((8, width), f32)),
        (const(3, 8, width), out((3, 8, width), f32)),
        (const(2, width, LANES), out((2, width, LANES), bf16)), (const(2, LANES, width), out((2, LANES, width), bf16)),
        (const(ntask, params[2].shape[1]), out((ntask, params[2].shape[1]), f32)),
        (const(ntask, params[0].shape[1]), out((ntask, params[0].shape[1]), f32)),
        (act, out(wide, bf16)), (act, out(wide, bf16)), (act, out(wide, bf16)), (act, out(wide, bf16)),
        (act, out(wide, f32)), (act, out(wide, bf16)), (act, out(wide, bf16)), (nar, out((rows, seq, LANES), f32)),
        (act, out(wide, f32)),
        (act, out(wide, bf16)), (act, out(wide, bf16)), (act, out(wide, bf16)), (act, out(wide, bf16)),
        (act, out(wide, f32)), (act, out(wide, bf16)),
        (any_spec, out((rows, heads, seq, seq), bf16)), (any_spec, out((rows, heads, seq, seq), bf16)),
    ]
    return pl.pallas_call(
        functools.partial(forward_kernel, lax.axis_size("dp"), ntask),
        grid=(rows,),
        in_specs=[
            pl.BlockSpec(memory_space=pltpu.SMEM), act, act,
            const(rows, seq), act,
        ] + [full(*item.shape) for item in params],
        out_specs=[spec for spec, _ in outs],
        out_shape=[shape for _, shape in outs],
        scratch_shapes=[
            pltpu.VMEM((64, LANES), f32), pltpu.VMEM((seq, seq), f32), pltpu.VMEM((2, 2, seq, seq), bf16),
            pltpu.SemaphoreType.DMA((2,)), pltpu.VMEM((seq, ff), bf16), pltpu.VMEM((seq, ff), f32),
            pltpu.VMEM((seq, width), f32),
            pltpu.VMEM((width, ff), f32), pltpu.VMEM((ff, width), f32), pltpu.SemaphoreType.DMA((4,)),
        ],
        cost_estimate=SHORT,
        compiler_params=pltpu.CompilerParams(vmem_limit_bytes=60 << 20),
    )(group_sizes, tokens, memory, segments, cotangent, *params)


def attend_back(q_ref, k_ref, v_ref, mixed_ref, share_ref, prob_ref, d_mixed_ref, masked, dq_ref, dk_ref, dv_ref):
    low = low_lanes()
    for pair in range(PAIRS):
        lanes = slice(pair * LANES, (pair + 1) * LANES)
        grad = d_mixed_ref[:, lanes].astype(f32) * share_ref[0, :, lanes]
        product = grad * mixed_ref[0, :, lanes].astype(f32)
        grad = grad.astype(bf16)
        q, k, v = q_ref[0, :, lanes], k_ref[0, :, lanes], v_ref[0, :, lanes]
        zero = jnp.zeros_like(q)
        dq = [None, None]
        whole = [None, None]
        half = [None, None]
        add = lambda old, new: new if old is None else old + new
        for head in range(2):
            own = low if head == 0 else jnp.logical_not(low)
            delta = jnp.sum(jnp.where(own, product, 0.0), axis=-1, keepdims=True)
            head_g, head_q, head_k = (jnp.where(own, item, zero) for item in (grad, q, k))
            for block in range(2):
                rows = slice(block * 256, (block + 1) * 256)
                span = (block + 1) * 256 if masked else 512
                prob = prob_ref[0, pair * 2 + head, rows, :span]
                d_prob = dot_nt(head_g[rows], v[:span])
                d_score = (prob.astype(f32) * (d_prob - delta[rows])).astype(bf16)
                dq[block] = add(dq[block], dot(d_score, head_k[:span]))
                kind = half if span == 256 else whole
                kind[0] = add(kind[0], dot_tn(head_q[rows], d_score))
                kind[1] = add(kind[1], dot_tn(head_g[rows], prob))
        for block in range(2):
            dq_ref[block * 256 : (block + 1) * 256, lanes] = (dq[block] * 0.125).astype(bf16)
        for out_ref, both, first in ((dk_ref, whole[0], half[0]), (dv_ref, whole[1], half[1])):
            if first is None:
                out_ref[:, lanes] = both.T.astype(bf16)
            else:
                out_ref[:256, lanes] = (both[:, :256] + first).T.astype(bf16)
                out_ref[256:, lanes] = both[:, 256:].T.astype(bf16)


def cross_back_kernel(
    grad_two_ref, mixed_ref, q_ref, k_ref, v_ref, share_ref, prob_ref, mem_ref, in_two_ref, after_one_ref,
    narrow_ref, branch_ref, gains_ref, down_w_ref, up_w_ref, cross_qkv_ref, cross_out_ref,
    kept_ref, sent_ref, mem_grad_ref, grad_one_ref, d_branch_ref, up_grad_ref, down_grad_ref, gain_grad_ref,
    d_mixed_ref, dq_ref, dk_ref, dv_ref, total_ref, part_sem,
):
    row = pl.program_id(0)

    @pl.when(row == 0)
    def _():
        for ref in (total_ref, up_grad_ref, down_grad_ref, gain_grad_ref):
            ref[...] = jnp.zeros_like(ref)

    grad_low = grad_two_ref[0].astype(bf16)
    total_ref[0:512] += dot_tn(mixed_ref[0], grad_low)
    d_mixed_ref[...] = dot_nt(grad_low, cross_out_ref[...]).astype(bf16)
    attend_back(q_ref, k_ref, v_ref, mixed_ref, share_ref, prob_ref, d_mixed_ref, False, dq_ref, dk_ref, dv_ref)
    total_ref[512:1024] += dot_tn(in_two_ref[0], dq_ref[...])
    memory_t = mem_ref[0].T
    total_ref[1024:1536] += dot(memory_t, dk_ref[...])
    total_ref[1536:2048] += dot(memory_t, dv_ref[...])

    @pl.when(row == pl.num_programs(0) - 1)
    def _():
        for copy in halves(total_ref, kept_ref, sent_ref, part_sem, 0):
            copy.start()

    mem_grad_ref[0] = dot_nt(dk_ref[...], cross_qkv_ref[1]) + dot_nt(dv_ref[...], cross_qkv_ref[2])
    d_in = dot_nt(dq_ref[...], cross_qkv_ref[0])
    after_one = after_one_ref[0]
    d_after, gain_grad = rms_back(after_one, rms_inv(after_one), gains_ref[1, 0:1], d_in)
    gain_grad_ref[...] += jnp.broadcast_to(gain_grad, gain_grad_ref.shape)
    grad = grad_two_ref[0] + d_after
    grad_one_ref[0] = grad
    grad_low = grad.astype(bf16)
    narrow = narrow_ref[0]
    gate = lax.logistic(narrow)
    narrow_act = (narrow * gate).astype(bf16)
    up_grad_ref[...] += dot_tn(narrow_act, grad_low)[:RANK]
    d_narrow = (dot_nt(grad_low, up_w_ref[0]) * (gate * (1.0 + narrow * (1.0 - gate)))).astype(bf16)
    down_grad_ref[...] += dot_tn(d_narrow, branch_ref[0])[:RANK]
    d_branch_ref[0] = (grad + dot_nt(d_narrow, down_w_ref[0])).astype(bf16)

    @pl.when(row == pl.num_programs(0) - 1)
    def _():
        for copy in halves(total_ref, kept_ref, sent_ref, part_sem, 0):
            copy.wait()


def self_back_kernel(
    d_branch_ref, mixed_ref, q_ref, k_ref, v_ref, share_ref, prob_ref, in_one_ref, x_ref, grad_one_ref, gains_ref,
    self_qkv_ref, self_out_ref,
    kept_ref, sent_ref, input_grad_ref, gain_grad_ref,
    d_mixed_ref, dq_ref, dk_ref, dv_ref, total_ref, part_sem,
):
    row = pl.program_id(0)

    @pl.when(row == 0)
    def _():
        for ref in (total_ref, gain_grad_ref):
            ref[...] = jnp.zeros_like(ref)

    total_ref[0:512] += dot_tn(mixed_ref[0], d_branch_ref[0])
    d_mixed_ref[...] = dot_nt(d_branch_ref[0], self_out_ref[...]).astype(bf16)
    attend_back(q_ref, k_ref, v_ref, mixed_ref, share_ref, prob_ref, d_mixed_ref, True, dq_ref, dk_ref, dv_ref)
    in_one_t = in_one_ref[0].T
    for j, ref in enumerate((dq_ref, dk_ref, dv_ref)):
        total_ref[(1 + j) * 512 : (2 + j) * 512] += dot(in_one_t, ref[...])

    @pl.when(row == pl.num_programs(0) - 1)
    def _():
        for copy in halves(total_ref, kept_ref, sent_ref, part_sem, 0):
            copy.start()

    d_in = None
    for j, ref in enumerate((dq_ref, dk_ref, dv_ref)):
        part = dot_nt(ref[...], self_qkv_ref[j])
        d_in = part if d_in is None else d_in + part
    x = x_ref[0].astype(f32)
    d_x, gain_grad = rms_back(x, rms_inv(x), gains_ref[0, 0:1], d_in)
    gain_grad_ref[...] += jnp.broadcast_to(gain_grad, gain_grad_ref.shape)
    input_grad_ref[0] = grad_one_ref[0] + d_x

    @pl.when(row == pl.num_programs(0) - 1)
    def _():
        for copy in halves(total_ref, kept_ref, sent_ref, part_sem, 0):
            copy.wait()


def small_kernel(
    ntask, sizes_ref, up_one_ref, up_two_ref, down_one_ref, down_two_ref, gain_one_ref, gain_two_ref, gain_three_ref,
    embed_ref, first_ref, second_ref, hgain_ref, hdown_ref, hup_ref, pre_ref,
    kept_ref, sent_ref, out_ref, flat_ref, fold_ref, part_sem,
):
    task, _ = task_place(sizes_ref, ntask, lax.axis_index("dp"))
    _, mine, fold = fold_tables()
    unfold = fold.astype(f32)
    pair_row = lax.broadcasted_iota(jnp.int32, (2 * ntask, LANES), 0)
    task_row = lax.broadcasted_iota(jnp.int32, (ntask, LANES), 0)
    for p, ref in enumerate((down_one_ref, down_two_ref)):
        tall = jnp.concatenate([ref[...], jnp.zeros((LANES - RANK, ref.shape[1]), f32)], axis=0).T
        spread = lax.dot_general(tall, unfold, (((1,), (1,)), ((), ())), precision=highest, preferred_element_type=f32)
        spread = jnp.where(mine, spread, 0.0)
        fold_ref[p] = jnp.sum(spread.reshape(64, 8, LANES), axis=1)
        for a in range(64):
            flat_ref[p : p + 1, a * LANES : (a + 1) * LANES] = fold_ref[p, a : a + 1]
        for a in range(RANK):
            flat_ref[2 + p : 3 + p, a * 512 : (a + 1) * 512] = (up_one_ref, up_two_ref)[p][a : a + 1, :]
    flat_ref[4:8, :] = jnp.zeros((4, flat_ref.shape[1]), f32)
    for a in range(64):
        lanes = slice((a % 4) * LANES, (a % 4 + 1) * LANES)
        r = a // 4
        for base, first_row, second_row in (
            (0, fold_ref[0, a : a + 1], fold_ref[1, a : a + 1]),
            (1024, up_one_ref[r : r + 1, lanes], up_two_ref[r : r + 1, lanes]),
        ):
            block = jnp.where(pair_row == 2 * task, first_row, jnp.where(pair_row == 2 * task + 1, second_row, 0.0))
            out_ref[base + a * 16 : base + (a + 1) * 16, :] = block
    gain = []
    for ref in (gain_one_ref, gain_two_ref, gain_three_ref):
        gain.append(ref[...])
    gain = jnp.concatenate(gain, axis=1)
    for j in range(12):
        block = jnp.where(task_row == task, gain[:, j * LANES : (j + 1) * LANES], 0.0)
        out_ref[2048 + j * 8 : 2056 + j * 8, :] = block
    flat = flat_ref[...]
    down_code = dot_exact_nt(flat, hdown_ref[...])
    up_code = dot_exact_nt(flat, hup_ref[...])
    d_codes = down_code[0:2] + up_code[2:4]
    d_code = d_codes[0:1] + d_codes[1:2] + dot_exact_nt(gain, hgain_ref[...])[0:1]
    one_row = lax.broadcasted_iota(jnp.int32, (8, 1), 0) == 0
    d_code = jnp.where(one_row, jnp.broadcast_to(d_code, (8, d_code.shape[1])), 0.0)
    pre = pick_row(pre_ref[...], task)
    embed = pick_row(embed_ref[...].astype(f32), task)
    hidden = jnp.broadcast_to(pre * lax.logistic(pre), (8, pre.shape[1]))
    exact_tn = lambda left, right: lax.dot_general(
        left, right, (((0,), (0,)), ((), ())), precision=highest, preferred_element_type=f32
    )
    own_second = exact_tn(hidden, d_code)
    d_pre = silu_back(pre, dot_exact(d_code, second_ref[...]))
    own_first = exact_tn(jnp.broadcast_to(embed, (8, embed.shape[1])), d_pre)
    own_task = dot_exact_nt(d_pre, first_ref[...])[0:1]
    rows = lax.broadcasted_iota(jnp.int32, (8, own_task.shape[1]), 0)
    task_block = jnp.where(rows == task, own_task, 0.0)
    code_block = jnp.where(rows == 0, d_codes[0:1], jnp.where(rows == 1, d_codes[1:2], 0.0))
    out_ref[2144:2208, :] = own_first
    out_ref[2208:2336, :] = jnp.concatenate([own_second, jnp.zeros_like(own_second)], axis=1)
    out_ref[2336:2344, :] = jnp.concatenate([task_block, code_block], axis=1)
    out_ref[2344:, :] = jnp.zeros((out_ref.shape[0] - 2344, LANES), f32)
    copies = halves(out_ref, kept_ref, sent_ref, part_sem, 0)
    for copy in copies:
        copy.start()
    for copy in copies:
        copy.wait()


def spread_kernel(
    ntask, sum_ref, code_ref, position_ref,
    task_ref, pos_ref, first_ref, second_ref, gain_ref, down_ref, up_ref,
):
    code = code_ref[...]
    emb = code.shape[1]
    position = position_ref[...].astype(f32)
    codes = jnp.stack([code + position[0:1], code + position[1:2]], axis=1).reshape(2 * ntask, emb)
    exact_tn = lambda left, right: lax.dot_general(
        left, right, (((0,), (0,)), ((), ())), precision=highest, preferred_element_type=f32
    )
    wide = lambda base, count, step: jnp.concatenate(
        [sum_ref[base + a * step : base + (a + 1) * step, :] for a in range(count)], axis=1
    )
    down_ref[...] = exact_tn(codes, wide(0, 64, 16))
    up_ref[...] = exact_tn(codes, wide(1024, 64, 16))
    gain_ref[...] = exact_tn(code, wide(2048, 12, 8))
    first_ref[...] = sum_ref[2144:2208, :]
    second_ref[...] = sum_ref[2208:2336, :emb]
    task_ref[...] = sum_ref[2336:2344, :emb]
    pos_ref[...] = sum_ref[2336:2338, emb:]


def call_rows(kernel, rows, ins, outs, scratch, limit=60):
    def spec(item, blocked):
        if blocked is None:
            return pl.BlockSpec(memory_space=pl.ANY)
        shape = item.shape
        if blocked:
            return pl.BlockSpec((1,) + tuple(shape[1:]), lambda r: (r,) + (0,) * (len(shape) - 1))
        return pl.BlockSpec(tuple(shape), lambda r: (0,) * len(shape))

    return pl.pallas_call(
        kernel,
        grid=(rows,),
        in_specs=[spec(*item) for item in ins],
        out_specs=[spec(*item) for item in outs],
        out_shape=[item for item, _ in outs],
        scratch_shapes=scratch,
        cost_estimate=SHORT,
        compiler_params=pltpu.CompilerParams(vmem_limit_bytes=limit << 20),
    )(*[item for item, _ in ins])


def add_kernel(bits, kept_ref, got_ref, sent_ref, next_ref):
    half = sent_ref.shape[0]
    side = upper(lax.axis_index("dp"), bits)
    theirs = pl.ds(pl.multiple_of((1 - side) * half, half), half)
    mine = pl.ds(pl.multiple_of(side * half, half), half)
    sent_ref[...] = kept_ref[theirs] + got_ref[theirs]
    next_ref[...] = kept_ref[mine] + got_ref[mine]


def join_kernel(bits, cuts, own_ref, got_ref, *refs):
    *out_refs, sem = refs
    half = own_ref.shape[0]
    side = upper(lax.axis_index("dp"), bits)

    def copies(low_ref, high_ref):
        found, at = [], 0
        for cut, out_ref in zip(cuts, out_refs):
            for source, first in ((low_ref, 0), (high_ref, half)):
                low, high = max(at, first), min(at + cut, first + half)
                if low < high:
                    found.append((source.at[pl.ds(low - first, high - low)], out_ref.at[pl.ds(low - at, high - low)]))
            at += cut
        return [pltpu.make_async_copy(*pair, sem.at[i]) for i, pair in enumerate(found)]

    for place, refs in ((0, (own_ref, got_ref)), (1, (got_ref, own_ref))):

        @pl.when(side == place)
        def _():
            every = copies(*refs)
            for copy in every:
                copy.start()
            for copy in every:
                copy.wait()


def add_parts(kept, got, bits):
    half = jax.ShapeDtypeStruct((kept.shape[0] // 2,) + kept.shape[1:], f32)
    return pl.pallas_call(
        functools.partial(add_kernel, bits),
        out_shape=[half, half],
        cost_estimate=SHORT,
        compiler_params=pltpu.CompilerParams(vmem_limit_bytes=16 << 20),
    )(kept, got)


def join_parts(own, got, bits, cuts):
    any_spec = pl.BlockSpec(memory_space=pl.ANY)
    return pl.pallas_call(
        functools.partial(join_kernel, bits, cuts),
        in_specs=[any_spec] * 2,
        out_specs=[any_spec] * len(cuts),
        out_shape=[jax.ShapeDtypeStruct((cut,) + own.shape[1:], f32) for cut in cuts],
        scratch_shapes=[pltpu.SemaphoreType.DMA((2 + len(cuts),))],
        cost_estimate=SHORT,
        compiler_params=pltpu.CompilerParams(vmem_limit_bytes=1 << 20),
    )(own, got)


SEQUENCE = "01A012B0213C03442013014203410234102013243142134223434D"
ORDER = ((1, 1), (2, 4), (4, 2), (8, 8), (16, 16))


class Line:
    def __init__(self):
        self.last = None

    def tie(self, values):
        if self.last is None:
            return values
        values, self.last["kept"] = lax.optimization_barrier((values, self.last["kept"]))
        return values


def summing(kept, sent, cuts, line, found):
    devices = lax.axis_size("dp")
    state = {}

    def swap(values, bits):
        moves = [(i, i ^ bits[i % 2]) for i in range(devices)]
        return lax.ppermute(values, "dp", moves)

    def mark(value):
        state["kept"] = value
        line.last = state

    high = [(32 << i, 32 << i) for i in range(max(devices // 32, 1).bit_length() - 1)]
    sent = line.tie(sent)
    got = swap(sent, ORDER[0])
    mark(kept)
    yield
    for bits in ORDER[1:-1]:
        got = line.tie(got)
        sent, kept = add_parts(state["kept"], got, bits)
        got = swap(sent, bits)
        mark(kept)
        yield
    for bits in list(ORDER[-1:]) + high:
        got = line.tie(got)
        total = state["kept"] + got
        got = swap(total, bits)
        mark(total)
        yield
    got = line.tie(got)
    total = state["kept"] + got
    for bits in ORDER[:-1][::-1]:
        got = swap(total, bits)
        mark(total)
        yield
        got = line.tie(got)
        own = state["kept"]
        if bits == ORDER[0]:
            break
        (total,) = join_parts(own, got, bits, (2 * own.shape[0],))
    parts = join_parts(own, got, ORDER[0], cuts)
    mark(parts[-1])
    found.append((parts[:-1], state))


def on_device(
    tokens, memory, segments, cotangent, group_sizes, task_embed, position_embed, hyper_first, hyper_second,
    hyper_gain, hyper_down, hyper_up, self_qkv, self_out, cross_qkv, cross_out, ffn_in, ffn_out,
):
    rows, seq, width = tokens.shape
    ntask = group_sizes.shape[0]
    hyper_second_t = hyper_second.T
    params = (
        task_embed, position_embed, hyper_first, hyper_second_t, hyper_gain, hyper_down, hyper_up,
        self_qkv, self_out, cross_qkv, cross_out, ffn_in, ffn_out,
    )
    (
        output, grad_two, in_kept, in_sent, out_kept, out_sent, up_two, down_two, gain_three,
        gains, down_w, up_w, pre, code,
        in_one, q_one, k_one, v_one, share_one, mixed_one, branch, narrow, after_one,
        in_two, q_two, k_two, v_two, share_two, mixed_two, prob_one, prob_two,
    ) = run_forward(tokens, memory, segments, cotangent, group_sizes, params)
    like = lambda shape, dtype=f32: jax.ShapeDtypeStruct(shape, dtype)
    wide = tokens.shape
    row_scratch = [pltpu.VMEM((seq, width), bf16)] * 4
    row_scratch += [pltpu.VMEM((4 * width, width), f32), pltpu.SemaphoreType.DMA((2,))]
    pair = (2 * width, width)
    line = Line()
    sums = [[] for _ in range(5)]
    ff = ffn_out.shape[0]

    def start(which, kept, sent, cuts):
        return summing(kept, sent, cuts, line, sums[which])

    def mark(value):
        line.last = {"kept": value}
        return line.last

    chunks = {"0": start(0, out_kept, out_sent, (ff,)), "1": start(1, in_kept, in_sent, (width,))}
    for step in SEQUENCE:
        if step in chunks:
            next(chunks[step], None)
        elif step == "A":
            grad_two = line.tie(grad_two)
            cross_kept, cross_sent, memory_grad, grad_one, d_branch, up_one, down_one, gain_two = call_rows(
                cross_back_kernel,
                rows,
                [
                    (grad_two, True), (mixed_two, True), (q_two, True), (k_two, True), (v_two, True), (share_two, True),
                    (prob_two, True), (memory, True), (in_two, True), (after_one, True), (narrow, True), (branch, True),
                    (gains, False), (down_w, False), (up_w, False), (cross_qkv, False), (cross_out, False),
                ],
                [
                    (like(pair), None), (like(pair), None), (like(wide), True), (like(wide), True),
                    (like(wide, bf16), True), (like((RANK, width)), False), (like((RANK, width)), False), (like((8, width)), False),
                ],
                row_scratch,
            )
            memory_grad = mark(memory_grad)
            chunks["2"] = start(2, cross_kept, cross_sent, (width, 3 * width))
        elif step == "B":
            d_branch = line.tie(d_branch)
            self_kept, self_sent, input_grad, gain_one = call_rows(
                self_back_kernel,
                rows,
                [
                    (d_branch, True), (mixed_one, True), (q_one, True), (k_one, True), (v_one, True), (share_one, True),
                    (prob_one, True), (in_one, True), (tokens, True), (grad_one, True), (gains, False),
                    (self_qkv, False), (self_out, False),
                ],
                [(like(pair), None), (like(pair), None), (like(wide), True), (like((8, width)), False)],
                row_scratch,
            )
            input_grad = mark(input_grad)
            chunks["3"] = start(3, self_kept, self_sent, (width, 3 * width))
        elif step == "C":
            gain_one = line.tie(gain_one)
            small_kept, small_sent = pl.pallas_call(
                functools.partial(small_kernel, ntask),
                out_shape=[like((1280, LANES))] * 2,
                in_specs=[pl.BlockSpec(memory_space=pltpu.SMEM)] + [pl.BlockSpec(memory_space=pltpu.VMEM)] * 14,
                out_specs=[pl.BlockSpec(memory_space=pl.ANY)] * 2,
                scratch_shapes=[
                    pltpu.VMEM((2560, LANES), f32), pltpu.VMEM((8, 8192), f32), pltpu.VMEM((2, 64, LANES), f32),
                    pltpu.SemaphoreType.DMA((2,)),
                ],
                cost_estimate=SHORT,
        compiler_params=pltpu.CompilerParams(vmem_limit_bytes=32 << 20),
            )(
                group_sizes, up_one, up_two, down_one, down_two, gain_one, gain_two, gain_three,
                task_embed, hyper_first, hyper_second_t, hyper_gain, hyper_down, hyper_up, pre,
            )
            mark(small_kept)
            chunks["4"] = start(4, small_kept, small_sent, (2560,))
        else:
            for _ in chunks["4"]:
                pass
            sum_small = line.tie(sums[4][0][1]["kept"])
            task_grad, position_grad, first_grad, second_grad, gain_grad, down_grad, up_grad = pl.pallas_call(
                functools.partial(spread_kernel, ntask),
                out_shape=[
                    like(item.shape)
                    for item in (task_embed, position_embed, hyper_first, hyper_second, hyper_gain, hyper_down, hyper_up)
                ],
                cost_estimate=SHORT,
        compiler_params=pltpu.CompilerParams(vmem_limit_bytes=32 << 20),
            )(sum_small, code, position_embed)
            task_grad = mark(task_grad)
    for rest in chunks.values():
        for _ in rest:
            pass
    memory_grad, input_grad, task_grad = memory_grad["kept"], input_grad["kept"], task_grad["kept"]
    sum_out, sum_in, cross_qkv_grad, self_qkv_grad = (sums[i][0][1]["kept"] for i in range(4))
    cross_out_grad, self_out_grad = sums[2][0][0][0], sums[3][0][0][0]
    cross_qkv_grad = cross_qkv_grad.reshape(cross_qkv.shape)
    self_qkv_grad = self_qkv_grad.reshape(self_qkv.shape)
    return (
        output, input_grad, memory_grad, task_grad, position_grad, first_grad, second_grad, gain_grad, down_grad,
        up_grad, self_qkv_grad, self_out_grad, cross_qkv_grad, cross_out_grad, sum_in, sum_out,
    )


def solution(mesh):
    split = P("dp", None, None)
    return jax.shard_map(
        on_device,
        mesh=mesh,
        in_specs=(split, split, P("dp", None), split) + (P(),) * 14,
        out_specs=(split,) * 3 + (P(),) * 13,
        check_vma=False,
    )
```

```python
import functools

import jax
import jax.numpy as jnp
from jax import lax
from jax.experimental import pallas as pl
from jax.experimental.pallas import tpu as pltpu
from jax.sharding import PartitionSpec as P

PAIRS = 4
LANES = 128
RANK = 16
LOG2E = 1.4426950408889634
epsilon = 1e-06
highest = lax.Precision.HIGHEST
f32 = jnp.float32
bf16 = jnp.bfloat16
SHORT = pl.CostEstimate(flops=1, bytes_accessed=1, transcendentals=0)


def dot(left, right):
    return jnp.dot(left, right, preferred_element_type=f32)


def dot_nt(left, right):
    return lax.dot_general(left, right, (((1,), (1,)), ((), ())), preferred_element_type=f32)


def dot_tn(left, right):
    return lax.dot_general(left, right, (((0,), (0,)), ((), ())), preferred_element_type=f32)


def three(values):
    high = values.astype(bf16)
    rest = values - high.astype(f32)
    mid = rest.astype(bf16)
    return high, mid, (rest - mid.astype(f32)).astype(bf16)


def dot_exact(values, table):
    high, mid, low = three(values)
    return dot(high, table) + (dot(mid, table) + dot(low, table))


def dot_exact_nt(values, table):
    high, mid, low = three(values)
    return dot_nt(high, table) + (dot_nt(mid, table) + dot_nt(low, table))


def rms_back(values, inv, gain, grad):
    unit = values * inv
    scaled = grad * gain
    mean = jnp.mean(scaled * unit, axis=-1, keepdims=True)
    return inv * (scaled - unit * mean), jnp.sum(grad * unit, axis=0, keepdims=True)


def rms_inv(values):
    return lax.rsqrt(jnp.mean(values * values, axis=-1, keepdims=True) + epsilon)


def low_lanes():
    return lax.broadcasted_iota(jnp.int32, (1, LANES), 1) < 64


def silu_back(values, grad):
    gate = lax.logistic(values)
    return grad * (gate * (1.0 + values * (1.0 - gate)))


def task_place(sizes_ref, count, place):
    end, task = jnp.int32(0), jnp.int32(0)
    for i in range(count):
        end = end + sizes_ref[i]
        task = task + jnp.where(end <= place, 1, 0)
    size = sizes_ref[0]
    for i in range(1, count):
        size = jnp.where(task == i, sizes_ref[i], size)
    return task, size


def pick_row(table, task):
    rows = lax.broadcasted_iota(jnp.int32, table.shape, 0)
    return jnp.sum(jnp.where(rows == task, table, 0.0), axis=0, keepdims=True)


def fold_tables():
    feature = lax.broadcasted_iota(jnp.int32, (512, 64), 0)
    block = lax.broadcasted_iota(jnp.int32, (512, 64), 1)
    expand = jnp.where(feature // 8 == block, 1.0, 0.0).astype(bf16)
    feature = lax.broadcasted_iota(jnp.int32, (512, LANES), 0)
    lane = lax.broadcasted_iota(jnp.int32, (512, LANES), 1)
    own = (lane // RANK) == (feature % 8)
    row = lax.broadcasted_iota(jnp.int32, (LANES, LANES), 0)
    lane = lax.broadcasted_iota(jnp.int32, (LANES, LANES), 1)
    fold = jnp.where((row % RANK) == lane, 1.0, 0.0).astype(bf16)
    return expand, own, fold


def upper(place, bits):
    return lax.rem(jnp.where(lax.rem(place, 2) == 1, place // bits[1], place // bits[0]), 2)


def halves(total_ref, kept_ref, sent_ref, sem, base):
    half = total_ref.shape[0] // 2
    side = lax.rem(lax.axis_index("dp"), 2)
    return (
        pltpu.make_async_copy(total_ref.at[pl.ds(pl.multiple_of((1 - side) * half, half), half)], sent_ref, sem.at[base]),
        pltpu.make_async_copy(total_ref.at[pl.ds(pl.multiple_of(side * half, half), half)], kept_ref, sem.at[base + 1]),
    )


def attend_block(pair_q, keys, values_ones, bias):
    low = low_lanes()
    probs, mixed = [], []
    for head in range(2):
        own = low if head == 0 else jnp.logical_not(low)
        scores = dot_nt(jnp.where(own, pair_q, jnp.zeros_like(pair_q)), keys)
        if bias is not None:
            scores = scores + bias
        top = jnp.max(scores, axis=-1, keepdims=True)
        prob = jnp.exp2((scores - top) * LOG2E).astype(bf16)
        probs.append(prob)
        mixed.append(dot(prob, values_ones))
    total = jnp.where(low, mixed[0][:, LANES:], mixed[1][:, LANES:])
    share = 1.0 / total
    out = jnp.where(low, mixed[0][:, :LANES], mixed[1][:, :LANES]) * share
    return probs, out.astype(bf16), share


def hyper_tables(task, embed_ref, position_ref, first_ref, second_ref, gain_ref, down_ref, up_ref,
                 gains_ref, down_w_ref, up_w_ref, pre_ref, code_ref, flat_ref):
    pre = dot(embed_ref[...], first_ref[...])
    code = dot_exact_nt(pre * lax.logistic(pre), second_ref[...])
    pre_ref[...] = pre
    code_ref[...] = code
    own = pick_row(code, task)
    gain = dot_exact(jnp.broadcast_to(own, (8, own.shape[1])), gain_ref[...])
    for i in range(3):
        gains_ref[i] = 1.0 + gain[:, i * 512 : (i + 1) * 512]
    rows = lax.broadcasted_iota(jnp.int32, (8, own.shape[1]), 0)
    position = position_ref[...].astype(f32)
    codes = own + jnp.where(rows == 0, position[0:1], position[1:2])
    expand, mine, fold = fold_tables()
    flat = dot_exact(codes, down_ref[...])
    for p in range(2):
        for a in range(64):
            flat_ref[a : a + 1, :] = flat[p : p + 1, a * LANES : (a + 1) * LANES]
        spread = jnp.where(mine, dot(expand, flat_ref[...].astype(bf16)), 0.0)
        down_w_ref[p] = dot(spread.astype(bf16), fold).astype(bf16)
    flat = dot_exact(codes, up_ref[...])
    for p in range(2):
        flat_ref[...] = jnp.zeros_like(flat_ref)
        wide = []
        for a in range(RANK):
            wide.append(flat[p : p + 1, a * 512 : (a + 1) * 512])
        wide.append(jnp.zeros((LANES - RANK, 512), f32))
        up_w_ref[p] = jnp.concatenate(wide, axis=0).astype(bf16)


def forward_kernel(
    total_devices, ntask,
    sizes_ref, x_ref, mem_ref, seg_ref, cot_ref,
    embed_ref, position_ref, first_ref, second_ref, hgain_ref, hdown_ref, hup_ref,
    self_qkv_ref, self_out_ref, cross_qkv_ref, cross_out_ref, ffn_in_ref, ffn_out_ref,
    output_ref, grad_two_ref, in_kept_ref, in_sent_ref, out_kept_ref, out_sent_ref, up_grad_ref, down_grad_ref, gain_grad_ref,
    gains_ref, down_w_ref, up_w_ref, pre_ref, code_ref,
    in_one_ref, q_ref, k_ref, v_ref, share_one_ref, mixed_one_ref, branch_ref, narrow_ref, after_one_ref,
    in_two_ref, cq_ref, ck_ref, cv_ref, share_two_ref, mixed_two_ref, prob_one_ref, prob_two_ref,
    flat_ref, bias_ref, slot_ref, sem, inner_act_ref, slope_ref, after_two_ref,
    ffn_in_grad_ref, ffn_out_grad_ref, part_sem,
):
    row = pl.program_id(0)
    place = lax.axis_index("dp")
    task, size = task_place(sizes_ref, ntask, place)

    @pl.when(row == 0)
    def _():
        hyper_tables(task, embed_ref, position_ref, first_ref, second_ref, hgain_ref, hdown_ref, hup_ref,
                     gains_ref, down_w_ref, up_w_ref, pre_ref, code_ref, flat_ref)

    x = x_ref[0].astype(f32)
    in_one = (x * rms_inv(x) * gains_ref[0, 0:1]).astype(bf16)
    in_one_ref[0] = in_one
    q_ref[0] = (dot(in_one, self_qkv_ref[0]).astype(bf16).astype(f32) * 0.125).astype(bf16)
    k_ref[0] = dot(in_one, self_qkv_ref[1]).astype(bf16)
    v_ref[0] = dot(in_one, self_qkv_ref[2]).astype(bf16)
    memory = mem_ref[0]
    ck_ref[0] = dot(memory, cross_qkv_ref[1]).astype(bf16)
    cv_ref[0] = dot(memory, cross_qkv_ref[2]).astype(bf16)
    queries = lax.broadcasted_iota(jnp.int32, (512, 512), 0)
    keys = lax.broadcasted_iota(jnp.int32, (512, 512), 1)
    segment = seg_ref[pl.ds(row, 1), :].astype(f32)
    segment_q = jnp.broadcast_to(segment, (LANES, segment.shape[1])).T[:, 0:1]
    allowed = jnp.logical_and(keys <= queries, segment_q == segment)
    bias_ref[...] = jnp.where(allowed, 0.0, -1e9)

    def attend_row(q_ref, k_ref, v_ref, masked, mixed_ref, share_ref, prob_ref, before):
        copies = []
        for pair in range(PAIRS):
            lanes = slice(pair * LANES, (pair + 1) * LANES)
            slot = pair
            if before:
                before[pair].wait()
            pair_k = k_ref[0, :, lanes]
            pair_v = v_ref[0, :, lanes]
            ones = jnp.concatenate([pair_v, jnp.ones_like(pair_v)], axis=1)
            for block in range(2):
                rows = slice(block * 256, (block + 1) * 256)
                span = (block + 1) * 256 if masked else 512
                probs, mixed, share = attend_block(
                    q_ref[0, rows, lanes], pair_k[:span], ones[:span],
                    bias_ref[rows, :span] if masked else None,
                )
                for head in range(2):
                    slot_ref[slot, head, rows, :span] = probs[head]
                mixed_ref[0, rows, lanes] = mixed
                share_ref[0, rows, lanes] = share
            copy = pltpu.make_async_copy(
                slot_ref.at[slot], prob_ref.at[row, pl.ds(pair * 2, 2)], sem.at[slot]
            )
            copy.start()
            copies.append(copy)
        return copies

    copies = attend_row(q_ref, k_ref, v_ref, True, mixed_one_ref, share_one_ref, prob_one_ref, [])

    branch = dot(mixed_one_ref[0], self_out_ref[...])
    branch_low = branch.astype(bf16)
    branch_ref[0] = branch_low
    narrow = dot(branch_low, down_w_ref[0])
    narrow_ref[0] = narrow
    narrow_act = (narrow * lax.logistic(narrow)).astype(bf16)
    after_one = x_ref[0].astype(f32) + branch + dot(narrow_act, up_w_ref[0])
    after_one_ref[0] = after_one
    in_two = (after_one * rms_inv(after_one) * gains_ref[1, 0:1]).astype(bf16)
    in_two_ref[0] = in_two
    cq_ref[0] = (dot(in_two, cross_qkv_ref[0]).astype(bf16).astype(f32) * 0.125).astype(bf16)

    copies = attend_row(cq_ref, ck_ref, cv_ref, False, mixed_two_ref, share_two_ref, prob_two_ref, copies)

    after_two = after_one_ref[0] + dot(mixed_two_ref[0], cross_out_ref[...])
    after_two_ref[...] = after_two
    in_three = (after_two * rms_inv(after_two) * gains_ref[2, 0:1]).astype(bf16)
    outer = None
    for c in range(4):
        cols = slice(c * 512, (c + 1) * 512)
        inner = dot(in_three, ffn_in_ref[:, cols])
        phi = 0.5 * (1.0 + lax.erf(inner * 0.7071067811865476))
        slope_ref[:, cols] = phi + inner * jnp.exp2(inner * inner * (-0.5 * LOG2E)) * 0.3989422804014327
        act = (inner * phi).astype(bf16)
        inner_act_ref[:, cols] = act
        part = dot(act, ffn_out_ref[cols, :])
        outer = part if outer is None else outer + part
    outer_low = outer.astype(bf16)
    narrow = dot(outer_low, down_w_ref[1])
    gate = lax.logistic(narrow)
    narrow_act = (narrow * gate).astype(bf16)
    output_ref[0] = (after_two_ref[...] + outer + dot(narrow_act, up_w_ref[1])).astype(bf16)

    keep = jnp.where(row == 0, 0.0, 1.0)
    share = total_devices / (ntask * size.astype(f32))
    grad = cot_ref[0].astype(f32) * share
    grad_low = grad.astype(bf16)
    d_narrow = (dot_nt(grad_low, up_w_ref[1]) * (gate * (1.0 + narrow * (1.0 - gate)))).astype(bf16)
    d_outer = (grad + dot_nt(d_narrow, down_w_ref[1])).astype(bf16)

    @pl.when(row == 0)
    def _():
        up_grad_ref[...] = jnp.zeros_like(up_grad_ref)
        down_grad_ref[...] = jnp.zeros_like(down_grad_ref)
        gain_grad_ref[...] = jnp.zeros_like(gain_grad_ref)
        ffn_in_grad_ref[...] = jnp.zeros_like(ffn_in_grad_ref)
        ffn_out_grad_ref[...] = jnp.zeros_like(ffn_out_grad_ref)

    up_grad_ref[...] += dot_tn(narrow_act, grad_low)[:RANK]
    down_grad_ref[...] += dot_tn(d_narrow, outer_low)[:RANK]
    for c in range(4):
        cols = slice(c * 512, (c + 1) * 512)
        ffn_out_grad_ref[cols, :] += dot_tn(inner_act_ref[:, cols], d_outer)

    last = row == pl.num_programs(0) - 1

    @pl.when(last)
    def _():
        for copy in halves(ffn_out_grad_ref, out_kept_ref, out_sent_ref, part_sem, 0):
            copy.start()

    for copy in copies:
        copy.wait()
    in_three_t = in_three.T
    d_in = None
    for c in range(4):
        cols = slice(c * 512, (c + 1) * 512)
        d_inner = (dot_nt(d_outer, ffn_out_ref[cols, :]) * slope_ref[:, cols]).astype(bf16)
        ffn_in_grad_ref[:, cols] += dot(in_three_t, d_inner)
        part = dot_nt(d_inner, ffn_in_ref[:, cols])
        d_in = part if d_in is None else d_in + part

    @pl.when(last)
    def _():
        for copy in halves(ffn_in_grad_ref, in_kept_ref, in_sent_ref, part_sem, 2):
            copy.start()

    after_two = after_two_ref[...]
    d_after, gain_grad = rms_back(after_two, rms_inv(after_two), gains_ref[2, 0:1], d_in)
    grad_two_ref[0] = cot_ref[0].astype(f32) * share + d_after
    gain_grad_ref[...] += jnp.broadcast_to(gain_grad, gain_grad_ref.shape)

    @pl.when(last)
    def _():
        for copy in halves(ffn_out_grad_ref, out_kept_ref, out_sent_ref, part_sem, 0):
            copy.wait()
        for copy in halves(ffn_in_grad_ref, in_kept_ref, in_sent_ref, part_sem, 2):
            copy.wait()


def run_forward(tokens, memory, segments, cotangent, group_sizes, params):
    rows, seq, width = tokens.shape
    ff = params[-1].shape[0]
    ntask = group_sizes.shape[0]
    full = lambda *shape: pl.BlockSpec(shape, lambda r: (0,) * len(shape), pipeline_mode=pl.Buffered(1))
    const = lambda *shape: pl.BlockSpec(shape, lambda r: (0,) * len(shape))
    act = pl.BlockSpec((1, seq, width), lambda r: (r, 0, 0))
    nar = pl.BlockSpec((1, seq, LANES), lambda r: (r, 0, 0))
    out = lambda shape, dtype: jax.ShapeDtypeStruct(shape, dtype)
    wide = (rows, seq, width)
    any_spec = pl.BlockSpec(memory_space=pl.ANY)
    heads = 2 * PAIRS
    outs = [
        (act, out(wide, bf16)), (act, out(wide, f32)),
        (any_spec, out((width // 2, ff), f32)), (any_spec, out((width // 2, ff), f32)),
        (any_spec, out((ff // 2, width), f32)), (any_spec, out((ff // 2, width), f32)),
        (const(RANK, width), out((RANK, width), f32)), (const(RANK, width), out((RANK, width), f32)),
        (const(8, width), out((8, width), f32)),
        (const(3, 8, width), out((3, 8, width), f32)),
        (const(2, width, LANES), out((2, width, LANES), bf16)), (const(2, LANES, width), out((2, LANES, width), bf16)),
        (const(ntask, params[2].shape[1]), out((ntask, params[2].shape[1]), f32)),
        (const(ntask, params[0].shape[1]), out((ntask, params[0].shape[1]), f32)),
        (act, out(wide, bf16)), (act, out(wide, bf16)), (act, out(wide, bf16)), (act, out(wide, bf16)),
        (act, out(wide, f32)), (act, out(wide, bf16)), (act, out(wide, bf16)), (nar, out((rows, seq, LANES), f32)),
        (act, out(wide, f32)),
        (act, out(wide, bf16)), (act, out(wide, bf16)), (act, out(wide, bf16)), (act, out(wide, bf16)),
        (act, out(wide, f32)), (act, out(wide, bf16)),
        (any_spec, out((rows, heads, seq, seq), bf16)), (any_spec, out((rows, heads, seq, seq), bf16)),
    ]
    return pl.pallas_call(
        functools.partial(forward_kernel, lax.axis_size("dp"), ntask),
        grid=(rows,),
        in_specs=[
            pl.BlockSpec(memory_space=pltpu.SMEM), act, act,
            const(rows, seq), act,
        ] + [full(*item.shape) for item in params],
        out_specs=[spec for spec, _ in outs],
        out_shape=[shape for _, shape in outs],
        scratch_shapes=[
            pltpu.VMEM((64, LANES), f32), pltpu.VMEM((seq, seq), f32), pltpu.VMEM((PAIRS, 2, seq, seq), bf16),
            pltpu.SemaphoreType.DMA((PAIRS,)), pltpu.VMEM((seq, ff), bf16), pltpu.VMEM((seq, ff), f32),
            pltpu.VMEM((seq, width), f32),
            pltpu.VMEM((width, ff), f32), pltpu.VMEM((ff, width), f32), pltpu.SemaphoreType.DMA((4,)),
        ],
        cost_estimate=SHORT,
        compiler_params=pltpu.CompilerParams(vmem_limit_bytes=60 << 20),
    )(group_sizes, tokens, memory, segments, cotangent, *params)


def attend_back(q_ref, k_ref, v_ref, mixed_ref, share_ref, prob_ref, d_mixed_ref, masked, dq_ref, dk_ref, dv_ref):
    low = low_lanes()
    for pair in range(PAIRS):
        lanes = slice(pair * LANES, (pair + 1) * LANES)
        grad = d_mixed_ref[:, lanes].astype(f32) * share_ref[0, :, lanes]
        product = grad * mixed_ref[0, :, lanes].astype(f32)
        grad = grad.astype(bf16)
        q, k, v = q_ref[0, :, lanes], k_ref[0, :, lanes], v_ref[0, :, lanes]
        zero = jnp.zeros_like(q)
        dq = [None, None]
        whole = [None, None]
        half = [None, None]
        add = lambda old, new: new if old is None else old + new
        for head in range(2):
            own = low if head == 0 else jnp.logical_not(low)
            delta = jnp.sum(jnp.where(own, product, 0.0), axis=-1, keepdims=True)
            head_g, head_q, head_k = (jnp.where(own, item, zero) for item in (grad, q, k))
            for block in range(2):
                rows = slice(block * 256, (block + 1) * 256)
                span = (block + 1) * 256 if masked else 512
                prob = prob_ref[0, pair * 2 + head, rows, :span]
                d_prob = dot_nt(head_g[rows], v[:span])
                d_score = (prob.astype(f32) * (d_prob - delta[rows])).astype(bf16)
                dq[block] = add(dq[block], dot(d_score, head_k[:span]))
                kind = half if span == 256 else whole
                kind[0] = add(kind[0], dot_tn(head_q[rows], d_score))
                kind[1] = add(kind[1], dot_tn(head_g[rows], prob))
        for block in range(2):
            dq_ref[block * 256 : (block + 1) * 256, lanes] = (dq[block] * 0.125).astype(bf16)
        for out_ref, both, first in ((dk_ref, whole[0], half[0]), (dv_ref, whole[1], half[1])):
            if first is None:
                out_ref[:, lanes] = both.T.astype(bf16)
            else:
                out_ref[:256, lanes] = (both[:, :256] + first).T.astype(bf16)
                out_ref[256:, lanes] = both[:, 256:].T.astype(bf16)


def heads_back_kernel(
    masked, grad_ref, mixed_ref, q_ref, k_ref, v_ref, share_ref, prob_ref, out_ref,
    dq_ref, dk_ref, dv_ref, out_grad_ref, d_mixed_ref,
):
    @pl.when(pl.program_id(0) == 0)
    def _():
        out_grad_ref[...] = jnp.zeros_like(out_grad_ref)

    grad_low = grad_ref[0].astype(bf16)
    out_grad_ref[...] += dot_tn(mixed_ref[0], grad_low)
    d_mixed_ref[...] = dot_nt(grad_low, out_ref[...]).astype(bf16)
    attend_back(
        q_ref, k_ref, v_ref, mixed_ref, share_ref, prob_ref, d_mixed_ref, masked,
        dq_ref.at[0], dk_ref.at[0], dv_ref.at[0],
    )


def cross_back_kernel(
    grad_two_ref, dq_ref, dk_ref, dv_ref, out_grad_ref, mem_ref, in_two_ref, after_one_ref,
    narrow_ref, branch_ref, gains_ref, down_w_ref, up_w_ref, cross_qkv_ref,
    kept_ref, sent_ref, mem_grad_ref, grad_one_ref, d_branch_ref, up_grad_ref, down_grad_ref, gain_grad_ref,
    total_ref, part_sem,
):
    row = pl.program_id(0)
    last = row == pl.num_programs(0) - 1
    dq, dk, dv = dq_ref[0], dk_ref[0], dv_ref[0]
    memory_t = mem_ref[0].T
    terms = (dot_tn(in_two_ref[0], dq), dot(memory_t, dk), dot(memory_t, dv))

    @pl.when(row == 0)
    def _():
        for ref in (up_grad_ref, down_grad_ref, gain_grad_ref):
            ref[...] = jnp.zeros_like(ref)
        total_ref[:512] = out_grad_ref[...]
        for i, term in enumerate(terms):
            total_ref[(1 + i) * 512 : (2 + i) * 512] = term

    @pl.when(row > 0)
    def _():
        for i, term in enumerate(terms):
            total_ref[(1 + i) * 512 : (2 + i) * 512] += term

    @pl.when(last)
    def _():
        for copy in halves(total_ref, kept_ref, sent_ref, part_sem, 0):
            copy.start()

    mem_grad_ref[0] = dot_nt(dk, cross_qkv_ref[1]) + dot_nt(dv, cross_qkv_ref[2])
    d_in = dot_nt(dq, cross_qkv_ref[0])
    after_one = after_one_ref[0]
    d_after, gain_grad = rms_back(after_one, rms_inv(after_one), gains_ref[1, 0:1], d_in)
    gain_grad_ref[...] += jnp.broadcast_to(gain_grad, gain_grad_ref.shape)
    grad = grad_two_ref[0] + d_after
    grad_one_ref[0] = grad
    grad_low = grad.astype(bf16)
    narrow = narrow_ref[0]
    gate = lax.logistic(narrow)
    narrow_act = (narrow * gate).astype(bf16)
    up_grad_ref[...] += dot_tn(narrow_act, grad_low)[:RANK]
    d_narrow = (dot_nt(grad_low, up_w_ref[0]) * (gate * (1.0 + narrow * (1.0 - gate)))).astype(bf16)
    down_grad_ref[...] += dot_tn(d_narrow, branch_ref[0])[:RANK]
    d_branch_ref[0] = (grad + dot_nt(d_narrow, down_w_ref[0])).astype(bf16)

    @pl.when(last)
    def _():
        for copy in halves(total_ref, kept_ref, sent_ref, part_sem, 0):
            copy.wait()


def self_back_kernel(
    dq_ref, dk_ref, dv_ref, out_grad_ref, in_one_ref, x_ref, grad_one_ref, gains_ref, self_qkv_ref,
    kept_ref, sent_ref, input_grad_ref, gain_grad_ref,
    total_ref, part_sem,
):
    row = pl.program_id(0)
    last = row == pl.num_programs(0) - 1
    in_one_t = in_one_ref[0].T
    terms = [dot(in_one_t, ref[0]) for ref in (dq_ref, dk_ref, dv_ref)]

    @pl.when(row == 0)
    def _():
        gain_grad_ref[...] = jnp.zeros_like(gain_grad_ref)
        total_ref[:512] = out_grad_ref[...]
        for i, term in enumerate(terms):
            total_ref[(1 + i) * 512 : (2 + i) * 512] = term

    @pl.when(row > 0)
    def _():
        for i, term in enumerate(terms):
            total_ref[(1 + i) * 512 : (2 + i) * 512] += term

    @pl.when(last)
    def _():
        for copy in halves(total_ref, kept_ref, sent_ref, part_sem, 0):
            copy.start()

    d_in = None
    for j, ref in enumerate((dq_ref, dk_ref, dv_ref)):
        part = dot_nt(ref[0], self_qkv_ref[j])
        d_in = part if d_in is None else d_in + part
    x = x_ref[0].astype(f32)
    d_x, gain_grad = rms_back(x, rms_inv(x), gains_ref[0, 0:1], d_in)
    gain_grad_ref[...] += jnp.broadcast_to(gain_grad, gain_grad_ref.shape)
    input_grad_ref[0] = grad_one_ref[0] + d_x

    @pl.when(last)
    def _():
        for copy in halves(total_ref, kept_ref, sent_ref, part_sem, 0):
            copy.wait()


def small_kernel(
    ntask, sizes_ref, up_one_ref, up_two_ref, down_one_ref, down_two_ref, gain_one_ref, gain_two_ref, gain_three_ref,
    embed_ref, first_ref, second_ref, hgain_ref, hdown_ref, hup_ref, pre_ref,
    kept_ref, sent_ref, out_ref, flat_ref, fold_ref, part_sem,
):
    task, _ = task_place(sizes_ref, ntask, lax.axis_index("dp"))
    _, mine, fold = fold_tables()
    unfold = fold.astype(f32)
    pair_row = lax.broadcasted_iota(jnp.int32, (2 * ntask, LANES), 0)
    task_row = lax.broadcasted_iota(jnp.int32, (ntask, LANES), 0)
    for p, ref in enumerate((down_one_ref, down_two_ref)):
        tall = jnp.concatenate([ref[...], jnp.zeros((LANES - RANK, ref.shape[1]), f32)], axis=0).T
        spread = lax.dot_general(tall, unfold, (((1,), (1,)), ((), ())), precision=highest, preferred_element_type=f32)
        spread = jnp.where(mine, spread, 0.0)
        fold_ref[p] = jnp.sum(spread.reshape(64, 8, LANES), axis=1)
        for a in range(64):
            flat_ref[p : p + 1, a * LANES : (a + 1) * LANES] = fold_ref[p, a : a + 1]
        for a in range(RANK):
            flat_ref[2 + p : 3 + p, a * 512 : (a + 1) * 512] = (up_one_ref, up_two_ref)[p][a : a + 1, :]
    flat_ref[4:8, :] = jnp.zeros((4, flat_ref.shape[1]), f32)
    for a in range(64):
        lanes = slice((a % 4) * LANES, (a % 4 + 1) * LANES)
        r = a // 4
        for base, first_row, second_row in (
            (0, fold_ref[0, a : a + 1], fold_ref[1, a : a + 1]),
            (1024, up_one_ref[r : r + 1, lanes], up_two_ref[r : r + 1, lanes]),
        ):
            block = jnp.where(pair_row == 2 * task, first_row, jnp.where(pair_row == 2 * task + 1, second_row, 0.0))
            out_ref[base + a * 16 : base + (a + 1) * 16, :] = block
    gain = []
    for ref in (gain_one_ref, gain_two_ref, gain_three_ref):
        gain.append(ref[...])
    gain = jnp.concatenate(gain, axis=1)
    for j in range(12):
        block = jnp.where(task_row == task, gain[:, j * LANES : (j + 1) * LANES], 0.0)
        out_ref[2048 + j * 8 : 2056 + j * 8, :] = block
    flat = flat_ref[...]
    down_code = dot_exact_nt(flat, hdown_ref[...])
    up_code = dot_exact_nt(flat, hup_ref[...])
    d_codes = down_code[0:2] + up_code[2:4]
    d_code = d_codes[0:1] + d_codes[1:2] + dot_exact_nt(gain, hgain_ref[...])[0:1]
    one_row = lax.broadcasted_iota(jnp.int32, (8, 1), 0) == 0
    d_code = jnp.where(one_row, jnp.broadcast_to(d_code, (8, d_code.shape[1])), 0.0)
    pre = pick_row(pre_ref[...], task)
    embed = pick_row(embed_ref[...].astype(f32), task)
    hidden = jnp.broadcast_to(pre * lax.logistic(pre), (8, pre.shape[1]))
    exact_tn = lambda left, right: lax.dot_general(
        left, right, (((0,), (0,)), ((), ())), precision=highest, preferred_element_type=f32
    )
    own_second = exact_tn(hidden, d_code)
    d_pre = silu_back(pre, dot_exact(d_code, second_ref[...]))
    own_first = exact_tn(jnp.broadcast_to(embed, (8, embed.shape[1])), d_pre)
    own_task = dot_exact_nt(d_pre, first_ref[...])[0:1]
    rows = lax.broadcasted_iota(jnp.int32, (8, own_task.shape[1]), 0)
    task_block = jnp.where(rows == task, own_task, 0.0)
    code_block = jnp.where(rows == 0, d_codes[0:1], jnp.where(rows == 1, d_codes[1:2], 0.0))
    out_ref[2144:2208, :] = own_first
    out_ref[2208:2336, :] = jnp.concatenate([own_second, jnp.zeros_like(own_second)], axis=1)
    out_ref[2336:2344, :] = jnp.concatenate([task_block, code_block], axis=1)
    out_ref[2344:, :] = jnp.zeros((out_ref.shape[0] - 2344, LANES), f32)
    copies = halves(out_ref, kept_ref, sent_ref, part_sem, 0)
    for copy in copies:
        copy.start()
    for copy in copies:
        copy.wait()


def spread_kernel(
    ntask, sum_ref, code_ref, position_ref,
    task_ref, pos_ref, first_ref, second_ref, gain_ref, down_ref, up_ref,
):
    code = code_ref[...]
    emb = code.shape[1]
    position = position_ref[...].astype(f32)
    codes = jnp.stack([code + position[0:1], code + position[1:2]], axis=1).reshape(2 * ntask, emb)
    exact_tn = lambda left, right: lax.dot_general(
        left, right, (((0,), (0,)), ((), ())), precision=highest, preferred_element_type=f32
    )
    wide = lambda base, count, step: jnp.concatenate(
        [sum_ref[base + a * step : base + (a + 1) * step, :] for a in range(count)], axis=1
    )
    down_ref[...] = exact_tn(codes, wide(0, 64, 16))
    up_ref[...] = exact_tn(codes, wide(1024, 64, 16))
    gain_ref[...] = exact_tn(code, wide(2048, 12, 8))
    first_ref[...] = sum_ref[2144:2208, :]
    second_ref[...] = sum_ref[2208:2336, :emb]
    task_ref[...] = sum_ref[2336:2344, :emb]
    pos_ref[...] = sum_ref[2336:2338, emb:]


def call_rows(kernel, rows, ins, outs, scratch, limit=60):
    def spec(item, blocked):
        if blocked is None:
            return pl.BlockSpec(memory_space=pl.ANY)
        shape = item.shape
        if blocked:
            return pl.BlockSpec((1,) + tuple(shape[1:]), lambda r: (r,) + (0,) * (len(shape) - 1))
        return pl.BlockSpec(tuple(shape), lambda r: (0,) * len(shape))

    return pl.pallas_call(
        kernel,
        grid=(rows,),
        in_specs=[spec(*item) for item in ins],
        out_specs=[spec(*item) for item in outs],
        out_shape=[item for item, _ in outs],
        scratch_shapes=scratch,
        cost_estimate=SHORT,
        compiler_params=pltpu.CompilerParams(vmem_limit_bytes=limit << 20),
    )(*[item for item, _ in ins])


def add_kernel(bits, kept_ref, got_ref, sent_ref, next_ref):
    half = sent_ref.shape[0]
    side = upper(lax.axis_index("dp"), bits)
    theirs = pl.ds(pl.multiple_of((1 - side) * half, half), half)
    mine = pl.ds(pl.multiple_of(side * half, half), half)
    sent_ref[...] = kept_ref[theirs] + got_ref[theirs]
    next_ref[...] = kept_ref[mine] + got_ref[mine]


def join_kernel(bits, cuts, own_ref, got_ref, *refs):
    *out_refs, sem = refs
    half = own_ref.shape[0]
    side = upper(lax.axis_index("dp"), bits)

    def copies(low_ref, high_ref):
        found, at = [], 0
        for cut, out_ref in zip(cuts, out_refs):
            for source, first in ((low_ref, 0), (high_ref, half)):
                low, high = max(at, first), min(at + cut, first + half)
                if low < high:
                    found.append((source.at[pl.ds(low - first, high - low)], out_ref.at[pl.ds(low - at, high - low)]))
            at += cut
        return [pltpu.make_async_copy(*pair, sem.at[i]) for i, pair in enumerate(found)]

    for place, refs in ((0, (own_ref, got_ref)), (1, (got_ref, own_ref))):

        @pl.when(side == place)
        def _():
            every = copies(*refs)
            for copy in every:
                copy.start()
            for copy in every:
                copy.wait()


def add_parts(kept, got, bits):
    half = jax.ShapeDtypeStruct((kept.shape[0] // 2,) + kept.shape[1:], f32)
    return pl.pallas_call(
        functools.partial(add_kernel, bits),
        out_shape=[half, half],
        cost_estimate=SHORT,
        compiler_params=pltpu.CompilerParams(vmem_limit_bytes=16 << 20),
    )(kept, got)


def join_parts(own, got, bits, cuts):
    any_spec = pl.BlockSpec(memory_space=pl.ANY)
    return pl.pallas_call(
        functools.partial(join_kernel, bits, cuts),
        in_specs=[any_spec] * 2,
        out_specs=[any_spec] * len(cuts),
        out_shape=[jax.ShapeDtypeStruct((cut,) + own.shape[1:], f32) for cut in cuts],
        scratch_shapes=[pltpu.SemaphoreType.DMA((2 + len(cuts),))],
        cost_estimate=SHORT,
        compiler_params=pltpu.CompilerParams(vmem_limit_bytes=1 << 20),
    )(own, got)


SEQUENCE = "A1001a0B1022b103C32014102423401323241340042433121243344D"
ORDERS = {
    "P": ((1, 1), (2, 4), (4, 2), (8, 8), (16, 16)),
    "Q": ((1, 1), (4, 2), (2, 4), (8, 8), (16, 16)),
    "R": ((1, 1), (4, 2), (8, 8), (16, 16), (2, 4)),
    "S": ((1, 1), (2, 4), (8, 8), (16, 16), (4, 2)),
}


class Line:
    def __init__(self):
        self.last = None

    def tie(self, values):
        if self.last is None:
            return values
        values, self.last["kept"] = lax.optimization_barrier((values, self.last["kept"]))
        return values


def summing(kept, sent, cuts, line, found, order):
    devices = lax.axis_size("dp")
    state = {}

    def swap(values, bits):
        moves = [(i, i ^ bits[i % 2]) for i in range(devices)]
        return lax.ppermute(values, "dp", moves)

    def mark(value):
        state["kept"] = value
        line.last = state

    high = [(32 << i, 32 << i) for i in range(max(devices // 32, 1).bit_length() - 1)]
    sent = line.tie(sent)
    got = swap(sent, order[0])
    mark(kept)
    yield
    for bits in order[1:-1]:
        got = line.tie(got)
        sent, kept = add_parts(state["kept"], got, bits)
        got = swap(sent, bits)
        mark(kept)
        yield
    for bits in list(order[-1:]) + high:
        got = line.tie(got)
        total = state["kept"] + got
        got = swap(total, bits)
        mark(total)
        yield
    got = line.tie(got)
    total = state["kept"] + got
    for bits in order[:-1][::-1]:
        got = swap(total, bits)
        mark(total)
        yield
        got = line.tie(got)
        own = state["kept"]
        if bits == order[0]:
            break
        (total,) = join_parts(own, got, bits, (2 * own.shape[0],))
    parts = join_parts(own, got, order[0], cuts)
    mark(parts[-1])
    found.append((parts[:-1], state))


def on_device(
    tokens, memory, segments, cotangent, group_sizes, task_embed, position_embed, hyper_first, hyper_second,
    hyper_gain, hyper_down, hyper_up, self_qkv, self_out, cross_qkv, cross_out, ffn_in, ffn_out,
):
    rows, seq, width = tokens.shape
    ntask = group_sizes.shape[0]
    hyper_second_t = hyper_second.T
    params = (
        task_embed, position_embed, hyper_first, hyper_second_t, hyper_gain, hyper_down, hyper_up,
        self_qkv, self_out, cross_qkv, cross_out, ffn_in, ffn_out,
    )
    (
        output, grad_two, in_kept, in_sent, out_kept, out_sent, up_two, down_two, gain_three,
        gains, down_w, up_w, pre, code,
        in_one, q_one, k_one, v_one, share_one, mixed_one, branch, narrow, after_one,
        in_two, q_two, k_two, v_two, share_two, mixed_two, prob_one, prob_two,
    ) = run_forward(tokens, memory, segments, cotangent, group_sizes, params)
    like = lambda shape, dtype=f32: jax.ShapeDtypeStruct(shape, dtype)
    wide = tokens.shape
    row_scratch = [pltpu.VMEM((seq, width), bf16)]
    total_scratch = [pltpu.VMEM((4 * width, width), f32), pltpu.SemaphoreType.DMA((2,))]
    pair = (2 * width, width)
    line = Line()
    sums = [[] for _ in range(5)]
    ff = ffn_out.shape[0]

    def start(which, kept, sent, cuts):
        return summing(kept, sent, cuts, line, sums[which], ORDERS["QQQQP"[which]])

    def mark(value):
        line.last = {"kept": value}
        return line.last

    chunks = {"0": start(0, out_kept, out_sent, (ff,)), "1": start(1, in_kept, in_sent, (width,))}
    for step in SEQUENCE:
        if step in chunks:
            next(chunks[step], None)
        elif step == "A":
            grad_two = line.tie(grad_two)
            dq, dk, dv, out_grad = call_rows(
                functools.partial(heads_back_kernel, False),
                rows,
                [
                    (grad_two, True), (mixed_two, True), (q_two, True), (k_two, True), (v_two, True),
                    (share_two, True), (prob_two, True), (cross_out, False),
                ],
                [(like(wide, bf16), True)] * 3 + [(like(cross_out.shape), False)],
                row_scratch,
            )
            held = mark(dq)
        elif step == "a":
            dq = line.tie(held["kept"])
            cross_kept, cross_sent, memory_grad, grad_one, d_branch, up_one, down_one, gain_two = call_rows(
                cross_back_kernel,
                rows,
                [
                    (grad_two, True), (dq, True), (dk, True), (dv, True), (out_grad, False), (memory, True),
                    (in_two, True), (after_one, True), (narrow, True), (branch, True),
                    (gains, False), (down_w, False), (up_w, False), (cross_qkv, False),
                ],
                [
                    (like(pair), None), (like(pair), None), (like(wide), True), (like(wide), True), (like(wide, bf16), True),
                    (like((RANK, width)), False), (like((RANK, width)), False), (like((8, width)), False),
                ],
                total_scratch,
            )
            memory_grad = mark(memory_grad)
            chunks["2"] = start(2, cross_kept, cross_sent, (width, 3 * width))
        elif step == "B":
            d_branch = line.tie(d_branch)
            dq, dk, dv, out_grad = call_rows(
                functools.partial(heads_back_kernel, True),
                rows,
                [
                    (d_branch, True), (mixed_one, True), (q_one, True), (k_one, True), (v_one, True),
                    (share_one, True), (prob_one, True), (self_out, False),
                ],
                [(like(wide, bf16), True)] * 3 + [(like(self_out.shape), False)],
                row_scratch,
            )
            held = mark(dq)
        elif step == "b":
            dq = line.tie(held["kept"])
            self_kept, self_sent, input_grad, gain_one = call_rows(
                self_back_kernel,
                rows,
                [
                    (dq, True), (dk, True), (dv, True), (out_grad, False), (in_one, True), (tokens, True),
                    (grad_one, True), (gains, False), (self_qkv, False),
                ],
                [(like(pair), None), (like(pair), None), (like(wide), True), (like((8, width)), False)],
                total_scratch,
            )
            input_grad = mark(input_grad)
            chunks["3"] = start(3, self_kept, self_sent, (width, 3 * width))
        elif step == "C":
            gain_one = line.tie(gain_one)
            small_kept, small_sent = pl.pallas_call(
                functools.partial(small_kernel, ntask),
                out_shape=[like((1280, LANES))] * 2,
                in_specs=[pl.BlockSpec(memory_space=pltpu.SMEM)] + [pl.BlockSpec(memory_space=pltpu.VMEM)] * 14,
                out_specs=[pl.BlockSpec(memory_space=pl.ANY)] * 2,
                scratch_shapes=[
                    pltpu.VMEM((2560, LANES), f32), pltpu.VMEM((8, 8192), f32), pltpu.VMEM((2, 64, LANES), f32),
                    pltpu.SemaphoreType.DMA((2,)),
                ],
                cost_estimate=SHORT,
        compiler_params=pltpu.CompilerParams(vmem_limit_bytes=32 << 20),
            )(
                group_sizes, up_one, up_two, down_one, down_two, gain_one, gain_two, gain_three,
                task_embed, hyper_first, hyper_second_t, hyper_gain, hyper_down, hyper_up, pre,
            )
            mark(small_kept)
            chunks["4"] = start(4, small_kept, small_sent, (2560,))
        else:
            for _ in chunks["4"]:
                pass
            sum_small = line.tie(sums[4][0][1]["kept"])
            task_grad, position_grad, first_grad, second_grad, gain_grad, down_grad, up_grad = pl.pallas_call(
                functools.partial(spread_kernel, ntask),
                out_shape=[
                    like(item.shape)
                    for item in (task_embed, position_embed, hyper_first, hyper_second, hyper_gain, hyper_down, hyper_up)
                ],
                cost_estimate=SHORT,
        compiler_params=pltpu.CompilerParams(vmem_limit_bytes=32 << 20),
            )(sum_small, code, position_embed)
            task_grad = mark(task_grad)
    for rest in chunks.values():
        for _ in rest:
            pass
    memory_grad, input_grad, task_grad = memory_grad["kept"], input_grad["kept"], task_grad["kept"]
    sum_out, sum_in, cross_qkv_grad, self_qkv_grad = (sums[i][0][1]["kept"] for i in range(4))
    cross_out_grad, self_out_grad = sums[2][0][0][0], sums[3][0][0][0]
    cross_qkv_grad = cross_qkv_grad.reshape(cross_qkv.shape)
    self_qkv_grad = self_qkv_grad.reshape(self_qkv.shape)
    return (
        output, input_grad, memory_grad, task_grad, position_grad, first_grad, second_grad, gain_grad, down_grad,
        up_grad, self_qkv_grad, self_out_grad, cross_qkv_grad, cross_out_grad, sum_in, sum_out,
    )


def solution(mesh):
    split = P("dp", None, None)
    return jax.shard_map(
        on_device,
        mesh=mesh,
        in_specs=(split, split, P("dp", None), split) + (P(),) * 14,
        out_specs=(split,) * 3 + (P(),) * 13,
        check_vma=False,
    )
```

```python
import functools

import jax
import jax.numpy as jnp
from jax import lax
from jax.experimental import pallas as pl
from jax.experimental.pallas import tpu as pltpu
from jax.sharding import PartitionSpec as P

PAIRS = 4
LANES = 128
RANK = 16
LOG2E = 1.4426950408889634
epsilon = 1e-06
highest = lax.Precision.HIGHEST
f32 = jnp.float32
bf16 = jnp.bfloat16
SHORT = pl.CostEstimate(flops=1, bytes_accessed=1, transcendentals=0)


def dot(left, right):
    return jnp.dot(left, right, preferred_element_type=f32)


def dot_nt(left, right):
    return lax.dot_general(left, right, (((1,), (1,)), ((), ())), preferred_element_type=f32)


def dot_tn(left, right):
    return lax.dot_general(left, right, (((0,), (0,)), ((), ())), preferred_element_type=f32)


def three(values):
    high = values.astype(bf16)
    rest = values - high.astype(f32)
    mid = rest.astype(bf16)
    return high, mid, (rest - mid.astype(f32)).astype(bf16)


def stacked(values):
    return jnp.concatenate([part.astype(f32) for part in three(values)], axis=0).astype(bf16)


def dot_exact(values, table):
    rows = values.shape[0]
    parts = dot(stacked(values), table)
    return parts[:rows] + (parts[rows : 2 * rows] + parts[2 * rows :])


def dot_exact_nt(values, table):
    rows = values.shape[0]
    parts = dot_nt(stacked(values), table)
    return parts[:rows] + (parts[rows : 2 * rows] + parts[2 * rows :])


def dot_exact_tn(left, right):
    l, r = three(left), three(right)
    pairs = ((0, 0), (0, 1), (0, 2), (1, 0), (1, 1), (2, 0))
    long = lambda parts, at: jnp.concatenate([parts[pair[at]].astype(f32) for pair in pairs], axis=0).astype(bf16)
    return dot_tn(long(l, 0), long(r, 1))


def rms_back(values, inv, gain, grad):
    unit = values * inv
    scaled = grad * gain
    mean = jnp.mean(scaled * unit, axis=-1, keepdims=True)
    return inv * (scaled - unit * mean), jnp.sum(grad * unit, axis=0, keepdims=True)


def rms_inv(values):
    return lax.rsqrt(jnp.mean(values * values, axis=-1, keepdims=True) + epsilon)


def low_lanes():
    return lax.broadcasted_iota(jnp.int32, (1, LANES), 1) < 64


def silu_back(values, grad):
    gate = lax.logistic(values)
    return grad * (gate * (1.0 + values * (1.0 - gate)))


def task_place(sizes_ref, count, place):
    end, task = jnp.int32(0), jnp.int32(0)
    for i in range(count):
        end = end + sizes_ref[i]
        task = task + jnp.where(end <= place, 1, 0)
    size = sizes_ref[0]
    for i in range(1, count):
        size = jnp.where(task == i, sizes_ref[i], size)
    return task, size


def pick_row(table, task):
    rows = lax.broadcasted_iota(jnp.int32, table.shape, 0)
    return jnp.sum(jnp.where(rows == task, table, 0.0), axis=0, keepdims=True)


def fold_tables():
    feature = lax.broadcasted_iota(jnp.int32, (512, 64), 0)
    block = lax.broadcasted_iota(jnp.int32, (512, 64), 1)
    expand = jnp.where(feature // 8 == block, 1.0, 0.0).astype(bf16)
    feature = lax.broadcasted_iota(jnp.int32, (512, LANES), 0)
    lane = lax.broadcasted_iota(jnp.int32, (512, LANES), 1)
    own = (lane // RANK) == (feature % 8)
    row = lax.broadcasted_iota(jnp.int32, (LANES, LANES), 0)
    lane = lax.broadcasted_iota(jnp.int32, (LANES, LANES), 1)
    fold = jnp.where((row % RANK) == lane, 1.0, 0.0).astype(bf16)
    return expand, own, fold


def upper(place, bits):
    return lax.rem(jnp.where(lax.rem(place, 2) == 1, place // bits[1], place // bits[0]), 2)


def halves(total_ref, kept_ref, sent_ref, sem, base):
    half = total_ref.shape[0] // 2
    side = lax.rem(lax.axis_index("dp"), 2)
    return (
        pltpu.make_async_copy(total_ref.at[pl.ds(pl.multiple_of((1 - side) * half, half), half)], sent_ref, sem.at[base]),
        pltpu.make_async_copy(total_ref.at[pl.ds(pl.multiple_of(side * half, half), half)], kept_ref, sem.at[base + 1]),
    )


def attend_block(pair_q, keys, values_ones, bias):
    low = low_lanes()
    probs, mixed = [], []
    for head in range(2):
        own = low if head == 0 else jnp.logical_not(low)
        scores = dot_nt(jnp.where(own, pair_q, jnp.zeros_like(pair_q)), keys)
        if bias is not None:
            scores = scores + bias
        top = jnp.max(scores, axis=-1, keepdims=True)
        prob = jnp.exp2((scores - top) * LOG2E).astype(bf16)
        probs.append(prob)
        mixed.append(dot(prob, values_ones))
    total = jnp.where(low, mixed[0][:, LANES:], mixed[1][:, LANES:])
    share = 1.0 / total
    out = jnp.where(low, mixed[0][:, :LANES], mixed[1][:, :LANES]) * share
    return probs, out.astype(bf16), share.astype(bf16)


def gain_tables(task, embed_ref, first_ref, second_ref, gain_ref, gains_ref, pre_ref, code_ref):
    pre = dot(embed_ref[...], first_ref[...])
    code = dot_exact_nt(pre * lax.logistic(pre), second_ref[...])
    pre_ref[...] = pre
    code_ref[...] = code
    own = pick_row(code, task)
    gain = dot_exact(jnp.broadcast_to(own, (8, own.shape[1])), gain_ref[...])
    for i in range(3):
        gains_ref[i] = 1.0 + gain[:, i * 512 : (i + 1) * 512]


def adapter_tables(task, position_ref, down_ref, up_ref, code_ref, down_w_ref, up_w_ref, flat_ref):
    own = pick_row(code_ref[...], task)
    rows = lax.broadcasted_iota(jnp.int32, (8, own.shape[1]), 0)
    position = position_ref[...].astype(f32)
    codes = own + jnp.where(rows == 0, position[0:1], position[1:2])
    expand, mine, fold = fold_tables()
    flat = dot_exact(codes, down_ref[...])
    for p in range(2):
        for a in range(64):
            flat_ref[a : a + 1, :] = flat[p : p + 1, a * LANES : (a + 1) * LANES]
        spread = jnp.where(mine, dot(expand, flat_ref[...].astype(bf16)), 0.0)
        down_w_ref[p] = dot(spread.astype(bf16), fold).astype(bf16)
    flat = dot_exact(codes, up_ref[...])
    for p in range(2):
        flat_ref[...] = jnp.zeros_like(flat_ref)
        wide = []
        for a in range(RANK):
            wide.append(flat[p : p + 1, a * 512 : (a + 1) * 512])
        wide.append(jnp.zeros((LANES - RANK, 512), f32))
        up_w_ref[p] = jnp.concatenate(wide, axis=0).astype(bf16)


def forward_kernel(
    total_devices, ntask,
    sizes_ref, x_ref, mem_ref, seg_ref, cot_ref,
    embed_ref, position_ref, first_ref, second_ref, hgain_ref, self_qkv_ref, *refs,
):
    weight_hbm, refs = refs[:7], refs[7:]
    (
    output_ref, grad_two_ref, in_kept_ref, in_sent_ref, out_kept_ref, out_sent_ref, up_grad_ref, down_grad_ref, gain_grad_ref,
    gains_ref, down_w_ref, up_w_ref, pre_ref, code_ref, prob_one_ref, prob_two_ref,
    ), keep_hbm, refs = refs[:16], refs[16:31], refs[31:]
    (
    flat_ref, bias_ref, slot_ref, sem, inner_act_ref, slope_ref, after_two_ref,
    ffn_in_grad_ref, ffn_out_grad_ref, part_sem, weight_sem, keep_sem,
    ), weight_refs, keep_refs = refs[:12], refs[12:19], refs[19:]
    row = pl.program_id(0)
    place = lax.axis_index("dp")
    task, size = task_place(sizes_ref, ntask, place)
    weights = [
        pltpu.make_async_copy(source, target, weight_sem.at[i])
        for i, (source, target) in enumerate(zip(weight_hbm, weight_refs))
    ]
    hdown_ref, hup_ref, self_out_ref, cross_qkv_ref, cross_out_ref, ffn_in_ref, ffn_out_ref = weight_refs
    (
        in_one_ref, q_ref, k_ref, v_ref, share_one_ref, mixed_one_ref, branch_ref, narrow_ref, after_one_ref,
        in_two_ref, cq_ref, ck_ref, cv_ref, share_two_ref, mixed_two_ref,
    ) = keep_refs
    keep = [
        pltpu.make_async_copy(source, target.at[pl.ds(row, 1)], keep_sem.at[i])
        for i, (source, target) in enumerate(zip(keep_refs, keep_hbm))
    ]

    def ready(*which):
        @pl.when(row == 0)
        def _():
            for i in which:
                weights[i].wait()

    def take_out(first, last):
        for copy in keep[first:last]:
            copy.start()

    @pl.when(row == 0)
    def _():
        for copy in weights:
            copy.start()
        gain_tables(task, embed_ref, first_ref, second_ref, hgain_ref, gains_ref, pre_ref, code_ref)

    x = x_ref[0].astype(f32)
    in_one = (x * rms_inv(x) * gains_ref[0, 0:1]).astype(bf16)
    in_one_ref[0] = in_one
    q_ref[0] = (dot(in_one, self_qkv_ref[0]).astype(bf16).astype(f32) * 0.125).astype(bf16)
    k_ref[0] = dot(in_one, self_qkv_ref[1]).astype(bf16)
    v_ref[0] = dot(in_one, self_qkv_ref[2]).astype(bf16)
    take_out(0, 4)
    queries = lax.broadcasted_iota(jnp.int32, (512, 512), 0)
    keys = lax.broadcasted_iota(jnp.int32, (512, 512), 1)
    segment = seg_ref[pl.ds(row, 1), :].astype(f32)
    segment_q = jnp.broadcast_to(segment, (LANES, segment.shape[1])).T[:, 0:1]
    allowed = jnp.logical_and(keys <= queries, segment_q == segment)
    bias_ref[...] = jnp.where(allowed, 0.0, -1e9)

    def attend_row(q_ref, k_ref, v_ref, masked, mixed_ref, share_ref, prob_ref, before):
        copies = []
        for pair in range(PAIRS):
            lanes = slice(pair * LANES, (pair + 1) * LANES)
            slot = pair
            if before:
                before[pair].wait()
            pair_k = k_ref[0, :, lanes]
            pair_v = v_ref[0, :, lanes]
            ones = jnp.concatenate([pair_v, jnp.ones_like(pair_v)], axis=1)
            for block in range(2):
                rows = slice(block * 256, (block + 1) * 256)
                span = (block + 1) * 256 if masked else 512
                probs, mixed, share = attend_block(
                    q_ref[0, rows, lanes], pair_k[:span], ones[:span],
                    bias_ref[rows, :span] if masked else None,
                )
                for head in range(2):
                    slot_ref[slot, head, rows, :span] = probs[head]
                mixed_ref[0, rows, lanes] = mixed
                share_ref[0, rows, lanes] = share
            copy = pltpu.make_async_copy(
                slot_ref.at[slot], prob_ref.at[row, pl.ds(pair * 2, 2)], sem.at[slot]
            )
            copy.start()
            copies.append(copy)
        return copies

    copies = attend_row(q_ref, k_ref, v_ref, True, mixed_one_ref, share_one_ref, prob_one_ref, [])
    take_out(4, 6)

    @pl.when(row == 0)
    def _():
        weights[0].wait()
        weights[1].wait()
        adapter_tables(task, position_ref, hdown_ref, hup_ref, code_ref, down_w_ref, up_w_ref, flat_ref)

    ready(2, 3, 4)
    memory = mem_ref[0]
    ck_ref[0] = dot(memory, cross_qkv_ref[1]).astype(bf16)
    cv_ref[0] = dot(memory, cross_qkv_ref[2]).astype(bf16)

    branch = dot(mixed_one_ref[0], self_out_ref[...])
    branch_low = branch.astype(bf16)
    branch_ref[0] = branch_low
    narrow = dot(branch_low, down_w_ref[0])
    narrow_ref[0] = narrow
    narrow_act = (narrow * lax.logistic(narrow)).astype(bf16)
    after_one = x_ref[0].astype(f32) + branch + dot(narrow_act, up_w_ref[0])
    after_one_ref[0] = after_one
    in_two = (after_one * rms_inv(after_one) * gains_ref[1, 0:1]).astype(bf16)
    in_two_ref[0] = in_two
    cq_ref[0] = (dot(in_two, cross_qkv_ref[0]).astype(bf16).astype(f32) * 0.125).astype(bf16)

    take_out(6, 13)
    copies = attend_row(cq_ref, ck_ref, cv_ref, False, mixed_two_ref, share_two_ref, prob_two_ref, copies)
    take_out(13, 15)
    ready(5, 6)

    after_two = after_one_ref[0] + dot(mixed_two_ref[0], cross_out_ref[...])
    after_two_ref[...] = after_two
    in_three = (after_two * rms_inv(after_two) * gains_ref[2, 0:1]).astype(bf16)
    outer = None
    for c in range(4):
        cols = slice(c * 512, (c + 1) * 512)
        inner = dot(in_three, ffn_in_ref[:, cols])
        phi = 0.5 * (1.0 + lax.erf(inner * 0.7071067811865476))
        slope_ref[:, cols] = phi + inner * jnp.exp2(inner * inner * (-0.5 * LOG2E)) * 0.3989422804014327
        act = (inner * phi).astype(bf16)
        inner_act_ref[:, cols] = act
        part = dot(act, ffn_out_ref[cols, :])
        outer = part if outer is None else outer + part
    outer_low = outer.astype(bf16)
    narrow = dot(outer_low, down_w_ref[1])
    gate = lax.logistic(narrow)
    narrow_act = (narrow * gate).astype(bf16)
    output_ref[0] = (after_two_ref[...] + outer + dot(narrow_act, up_w_ref[1])).astype(bf16)

    share = total_devices / (ntask * size.astype(f32))
    grad = cot_ref[0].astype(f32) * share
    grad_low = grad.astype(bf16)
    d_narrow = (dot_nt(grad_low, up_w_ref[1]) * (gate * (1.0 + narrow * (1.0 - gate)))).astype(bf16)
    d_outer = (grad + dot_nt(d_narrow, down_w_ref[1])).astype(bf16)

    @pl.when(row == 0)
    def _():
        up_grad_ref[...] = jnp.zeros_like(up_grad_ref)
        down_grad_ref[...] = jnp.zeros_like(down_grad_ref)
        gain_grad_ref[...] = jnp.zeros_like(gain_grad_ref)
        ffn_in_grad_ref[...] = jnp.zeros_like(ffn_in_grad_ref)
        ffn_out_grad_ref[...] = jnp.zeros_like(ffn_out_grad_ref)

    up_grad_ref[...] += dot_tn(narrow_act, grad_low)[:RANK]
    down_grad_ref[...] += dot_tn(d_narrow, outer_low)[:RANK]
    for c in range(4):
        cols = slice(c * 512, (c + 1) * 512)
        ffn_out_grad_ref[cols, :] += dot_tn(inner_act_ref[:, cols], d_outer)

    last = row == pl.num_programs(0) - 1

    @pl.when(last)
    def _():
        for copy in halves(ffn_out_grad_ref, out_kept_ref, out_sent_ref, part_sem, 0):
            copy.start()

    for copy in copies + keep:
        copy.wait()
    in_three_t = in_three.T
    d_in = None
    for c in range(4):
        cols = slice(c * 512, (c + 1) * 512)
        d_inner = (dot_nt(d_outer, ffn_out_ref[cols, :]) * slope_ref[:, cols]).astype(bf16)
        ffn_in_grad_ref[:, cols] += dot(in_three_t, d_inner)
        part = dot_nt(d_inner, ffn_in_ref[:, cols])
        d_in = part if d_in is None else d_in + part

    @pl.when(last)
    def _():
        for copy in halves(ffn_in_grad_ref, in_kept_ref, in_sent_ref, part_sem, 2):
            copy.start()

    after_two = after_two_ref[...]
    d_after, gain_grad = rms_back(after_two, rms_inv(after_two), gains_ref[2, 0:1], d_in)
    grad_two_ref[0] = cot_ref[0].astype(f32) * share + d_after
    gain_grad_ref[...] += jnp.broadcast_to(gain_grad, gain_grad_ref.shape)

    @pl.when(last)
    def _():
        for copy in halves(ffn_out_grad_ref, out_kept_ref, out_sent_ref, part_sem, 0):
            copy.wait()
        for copy in halves(ffn_in_grad_ref, in_kept_ref, in_sent_ref, part_sem, 2):
            copy.wait()


def run_forward(tokens, memory, segments, cotangent, group_sizes, params):
    rows, seq, width = tokens.shape
    ff = params[-1].shape[0]
    ntask = group_sizes.shape[0]
    full = lambda *shape: pl.BlockSpec(shape, lambda r: (0,) * len(shape), pipeline_mode=pl.Buffered(1))
    const = lambda *shape: pl.BlockSpec(shape, lambda r: (0,) * len(shape))
    act = pl.BlockSpec((1, seq, width), lambda r: (r, 0, 0))
    out = lambda shape, dtype: jax.ShapeDtypeStruct(shape, dtype)
    wide = (rows, seq, width)
    any_spec = pl.BlockSpec(memory_space=pl.ANY)
    heads = 2 * PAIRS
    outs = [
        (act, out(wide, bf16)), (act, out(wide, f32)),
        (any_spec, out((width // 2, ff), f32)), (any_spec, out((width // 2, ff), f32)),
        (any_spec, out((ff // 2, width), f32)), (any_spec, out((ff // 2, width), f32)),
        (const(RANK, width), out((RANK, width), f32)), (const(RANK, width), out((RANK, width), f32)),
        (const(8, width), out((8, width), f32)),
        (const(3, 8, width), out((3, 8, width), f32)),
        (const(2, width, LANES), out((2, width, LANES), bf16)), (const(2, LANES, width), out((2, LANES, width), bf16)),
        (const(ntask, params[2].shape[1]), out((ntask, params[2].shape[1]), f32)),
        (const(ntask, params[0].shape[1]), out((ntask, params[0].shape[1]), f32)),
        (any_spec, out((rows, heads, seq, seq), bf16)), (any_spec, out((rows, heads, seq, seq), bf16)),
    ]
    kept = [out(wide, bf16)] * 7 + [out((rows, seq, LANES), f32), out(wide, f32)] + [out(wide, bf16)] * 6
    outs += [(any_spec, item) for item in kept]
    early = params[:5] + params[7:8]
    late = params[5:7] + params[8:]
    return pl.pallas_call(
        functools.partial(forward_kernel, lax.axis_size("dp"), ntask),
        grid=(rows,),
        in_specs=[
            pl.BlockSpec(memory_space=pltpu.SMEM), act, act,
            const(rows, seq), act,
        ] + [full(*item.shape) for item in early] + [any_spec] * len(late),
        out_specs=[spec for spec, _ in outs],
        out_shape=[shape for _, shape in outs],
        scratch_shapes=[
            pltpu.VMEM((64, LANES), f32), pltpu.VMEM((seq, seq), f32), pltpu.VMEM((PAIRS, 2, seq, seq), bf16),
            pltpu.SemaphoreType.DMA((PAIRS,)), pltpu.VMEM((seq, ff), bf16), pltpu.VMEM((seq, ff), f32),
            pltpu.VMEM((seq, width), f32),
            pltpu.VMEM((width, ff), f32), pltpu.VMEM((ff, width), f32), pltpu.SemaphoreType.DMA((4,)),
            pltpu.SemaphoreType.DMA((len(late),)), pltpu.SemaphoreType.DMA((len(kept),)),
            *[pltpu.VMEM(item.shape, item.dtype) for item in late],
            *[pltpu.VMEM((1,) + item.shape[1:], item.dtype) for item in kept],
        ],
        cost_estimate=SHORT,
        compiler_params=pltpu.CompilerParams(vmem_limit_bytes=60 << 20),
    )(group_sizes, tokens, memory, segments, cotangent, *early, *late)


def attend_back(q_ref, k_ref, v_ref, mixed_ref, share_ref, prob_ref, d_mixed_ref, masked, dq_ref, dk_ref, dv_ref):
    low = low_lanes()
    for pair in range(PAIRS):
        lanes = slice(pair * LANES, (pair + 1) * LANES)
        grad = d_mixed_ref[:, lanes].astype(f32) * share_ref[0, :, lanes].astype(f32)
        product = grad * mixed_ref[0, :, lanes].astype(f32)
        grad = grad.astype(bf16)
        q, k, v = q_ref[0, :, lanes], k_ref[0, :, lanes], v_ref[0, :, lanes]
        zero = jnp.zeros_like(q)
        dq = [None, None]
        whole = [None, None]
        half = [None, None]
        add = lambda old, new: new if old is None else old + new
        for head in range(2):
            own = low if head == 0 else jnp.logical_not(low)
            delta = jnp.sum(jnp.where(own, product, 0.0), axis=-1, keepdims=True)
            head_g, head_q, head_k = (jnp.where(own, item, zero) for item in (grad, q, k))
            for block in range(2):
                rows = slice(block * 256, (block + 1) * 256)
                span = (block + 1) * 256 if masked else 512
                prob = prob_ref[0, pair * 2 + head, rows, :span]
                d_prob = dot_nt(head_g[rows], v[:span])
                d_score = (prob.astype(f32) * (d_prob - delta[rows])).astype(bf16)
                dq[block] = add(dq[block], dot(d_score, head_k[:span]))
                kind = half if span == 256 else whole
                kind[0] = add(kind[0], dot_tn(head_q[rows], d_score))
                kind[1] = add(kind[1], dot_tn(head_g[rows], prob))
        for block in range(2):
            dq_ref[block * 256 : (block + 1) * 256, lanes] = (dq[block] * 0.125).astype(bf16)
        for out_ref, both, first in ((dk_ref, whole[0], half[0]), (dv_ref, whole[1], half[1])):
            if first is None:
                out_ref[:, lanes] = both.T.astype(bf16)
            else:
                out_ref[:256, lanes] = (both[:, :256] + first).T.astype(bf16)
                out_ref[256:, lanes] = both[:, 256:].T.astype(bf16)


def heads_back_kernel(
    masked, grad_ref, mixed_ref, q_ref, k_ref, v_ref, share_ref, prob_ref, out_ref,
    dq_ref, dk_ref, dv_ref, out_grad_ref, d_mixed_ref,
):
    @pl.when(pl.program_id(0) == 0)
    def _():
        out_grad_ref[...] = jnp.zeros_like(out_grad_ref)

    grad_low = grad_ref[0].astype(bf16)
    out_grad_ref[...] += dot_tn(mixed_ref[0], grad_low)
    d_mixed_ref[...] = dot_nt(grad_low, out_ref[...]).astype(bf16)
    attend_back(
        q_ref, k_ref, v_ref, mixed_ref, share_ref, prob_ref, d_mixed_ref, masked,
        dq_ref.at[0], dk_ref.at[0], dv_ref.at[0],
    )


def cross_back_kernel(
    grad_two_ref, dq_ref, dk_ref, dv_ref, out_grad_ref, mem_ref, in_two_ref, after_one_ref,
    narrow_ref, branch_ref, gains_ref, down_w_ref, up_w_ref, cross_qkv_ref,
    kept_ref, sent_ref, mem_grad_ref, grad_one_ref, d_branch_ref, up_grad_ref, down_grad_ref, gain_grad_ref,
    total_ref, part_sem,
):
    row = pl.program_id(0)
    last = row == pl.num_programs(0) - 1
    dq, dk, dv = dq_ref[0], dk_ref[0], dv_ref[0]
    memory_t = mem_ref[0].T
    terms = (dot_tn(in_two_ref[0], dq), dot(memory_t, dk), dot(memory_t, dv))

    @pl.when(row == 0)
    def _():
        for ref in (up_grad_ref, down_grad_ref, gain_grad_ref):
            ref[...] = jnp.zeros_like(ref)
        total_ref[:512] = out_grad_ref[...]
        for i, term in enumerate(terms):
            total_ref[(1 + i) * 512 : (2 + i) * 512] = term

    @pl.when(row > 0)
    def _():
        for i, term in enumerate(terms):
            total_ref[(1 + i) * 512 : (2 + i) * 512] += term

    @pl.when(last)
    def _():
        for copy in halves(total_ref, kept_ref, sent_ref, part_sem, 0):
            copy.start()

    mem_grad_ref[0] = dot_nt(dk, cross_qkv_ref[1]) + dot_nt(dv, cross_qkv_ref[2])
    d_in = dot_nt(dq, cross_qkv_ref[0])
    after_one = after_one_ref[0]
    d_after, gain_grad = rms_back(after_one, rms_inv(after_one), gains_ref[1, 0:1], d_in)
    gain_grad_ref[...] += jnp.broadcast_to(gain_grad, gain_grad_ref.shape)
    grad = grad_two_ref[0] + d_after
    grad_one_ref[0] = grad
    grad_low = grad.astype(bf16)
    narrow = narrow_ref[0]
    gate = lax.logistic(narrow)
    narrow_act = (narrow * gate).astype(bf16)
    up_grad_ref[...] += dot_tn(narrow_act, grad_low)[:RANK]
    d_narrow = (dot_nt(grad_low, up_w_ref[0]) * (gate * (1.0 + narrow * (1.0 - gate)))).astype(bf16)
    down_grad_ref[...] += dot_tn(d_narrow, branch_ref[0])[:RANK]
    d_branch_ref[0] = (grad + dot_nt(d_narrow, down_w_ref[0])).astype(bf16)

    @pl.when(last)
    def _():
        for copy in halves(total_ref, kept_ref, sent_ref, part_sem, 0):
            copy.wait()


def self_back_kernel(
    dq_ref, dk_ref, dv_ref, out_grad_ref, in_one_ref, x_ref, grad_one_ref, gains_ref, self_qkv_ref,
    kept_ref, sent_ref, input_grad_ref, gain_grad_ref,
    total_ref, part_sem,
):
    row = pl.program_id(0)
    last = row == pl.num_programs(0) - 1
    in_one_t = in_one_ref[0].T
    terms = [dot(in_one_t, ref[0]) for ref in (dq_ref, dk_ref, dv_ref)]

    @pl.when(row == 0)
    def _():
        gain_grad_ref[...] = jnp.zeros_like(gain_grad_ref)
        total_ref[:512] = out_grad_ref[...]
        for i, term in enumerate(terms):
            total_ref[(1 + i) * 512 : (2 + i) * 512] = term

    @pl.when(row > 0)
    def _():
        for i, term in enumerate(terms):
            total_ref[(1 + i) * 512 : (2 + i) * 512] += term

    @pl.when(last)
    def _():
        for copy in halves(total_ref, kept_ref, sent_ref, part_sem, 0):
            copy.start()

    d_in = None
    for j, ref in enumerate((dq_ref, dk_ref, dv_ref)):
        part = dot_nt(ref[0], self_qkv_ref[j])
        d_in = part if d_in is None else d_in + part
    x = x_ref[0].astype(f32)
    d_x, gain_grad = rms_back(x, rms_inv(x), gains_ref[0, 0:1], d_in)
    gain_grad_ref[...] += jnp.broadcast_to(gain_grad, gain_grad_ref.shape)
    input_grad_ref[0] = grad_one_ref[0] + d_x

    @pl.when(last)
    def _():
        for copy in halves(total_ref, kept_ref, sent_ref, part_sem, 0):
            copy.wait()


def small_kernel(
    ntask, sizes_ref, up_one_ref, up_two_ref, down_one_ref, down_two_ref, gain_one_ref, gain_two_ref, gain_three_ref,
    embed_ref, first_ref, second_ref, hgain_ref, hdown_ref, hup_ref, pre_ref,
    kept_ref, sent_ref, out_ref, flat_ref, fold_ref, part_sem,
):
    task, _ = task_place(sizes_ref, ntask, lax.axis_index("dp"))
    _, mine, fold = fold_tables()
    unfold = fold.astype(f32)
    pair_row = lax.broadcasted_iota(jnp.int32, (2 * ntask, LANES), 0)
    task_row = lax.broadcasted_iota(jnp.int32, (ntask, LANES), 0)
    for p, ref in enumerate((down_one_ref, down_two_ref)):
        tall = jnp.concatenate([ref[...], jnp.zeros((LANES - RANK, ref.shape[1]), f32)], axis=0).T
        spread = lax.dot_general(tall, unfold, (((1,), (1,)), ((), ())), precision=highest, preferred_element_type=f32)
        spread = jnp.where(mine, spread, 0.0)
        fold_ref[p] = jnp.sum(spread.reshape(64, 8, LANES), axis=1)
        for a in range(64):
            flat_ref[p : p + 1, a * LANES : (a + 1) * LANES] = fold_ref[p, a : a + 1]
        for a in range(RANK):
            flat_ref[2 + p : 3 + p, a * 512 : (a + 1) * 512] = (up_one_ref, up_two_ref)[p][a : a + 1, :]
    flat_ref[4:8, :] = jnp.zeros((4, flat_ref.shape[1]), f32)
    for a in range(64):
        lanes = slice((a % 4) * LANES, (a % 4 + 1) * LANES)
        r = a // 4
        for base, first_row, second_row in (
            (0, fold_ref[0, a : a + 1], fold_ref[1, a : a + 1]),
            (1024, up_one_ref[r : r + 1, lanes], up_two_ref[r : r + 1, lanes]),
        ):
            block = jnp.where(pair_row == 2 * task, first_row, jnp.where(pair_row == 2 * task + 1, second_row, 0.0))
            out_ref[base + a * 16 : base + (a + 1) * 16, :] = block
    gain = []
    for ref in (gain_one_ref, gain_two_ref, gain_three_ref):
        gain.append(ref[...])
    gain = jnp.concatenate(gain, axis=1)
    for j in range(12):
        block = jnp.where(task_row == task, gain[:, j * LANES : (j + 1) * LANES], 0.0)
        out_ref[2048 + j * 8 : 2056 + j * 8, :] = block
    flat = flat_ref[...]
    down_code = dot_exact_nt(flat, hdown_ref[...])
    up_code = dot_exact_nt(flat, hup_ref[...])
    d_codes = down_code[0:2] + up_code[2:4]
    d_code = d_codes[0:1] + d_codes[1:2] + dot_exact_nt(gain, hgain_ref[...])[0:1]
    one_row = lax.broadcasted_iota(jnp.int32, (8, 1), 0) == 0
    d_code = jnp.where(one_row, jnp.broadcast_to(d_code, (8, d_code.shape[1])), 0.0)
    pre = pick_row(pre_ref[...], task)
    embed = pick_row(embed_ref[...].astype(f32), task)
    hidden = jnp.broadcast_to(pre * lax.logistic(pre), (8, pre.shape[1]))
    exact_tn = lambda left, right: lax.dot_general(
        left, right, (((0,), (0,)), ((), ())), precision=highest, preferred_element_type=f32
    )
    own_second = exact_tn(hidden, d_code)
    d_pre = silu_back(pre, dot_exact(d_code, second_ref[...]))
    own_first = exact_tn(jnp.broadcast_to(embed, (8, embed.shape[1])), d_pre)
    own_task = dot_exact_nt(d_pre, first_ref[...])[0:1]
    rows = lax.broadcasted_iota(jnp.int32, (8, own_task.shape[1]), 0)
    task_block = jnp.where(rows == task, own_task, 0.0)
    code_block = jnp.where(rows == 0, d_codes[0:1], jnp.where(rows == 1, d_codes[1:2], 0.0))
    out_ref[2144:2208, :] = own_first
    out_ref[2208:2336, :] = jnp.concatenate([own_second, jnp.zeros_like(own_second)], axis=1)
    out_ref[2336:2344, :] = jnp.concatenate([task_block, code_block], axis=1)
    out_ref[2344:, :] = jnp.zeros((out_ref.shape[0] - 2344, LANES), f32)
    copies = halves(out_ref, kept_ref, sent_ref, part_sem, 0)
    for copy in copies:
        copy.start()
    for copy in copies:
        copy.wait()


def spread_kernel(
    ntask, sum_ref, code_ref, position_ref,
    task_ref, pos_ref, first_ref, second_ref, gain_ref, down_ref, up_ref,
):
    code = code_ref[...]
    emb = code.shape[1]
    position = position_ref[...].astype(f32)
    codes = jnp.stack([code + position[0:1], code + position[1:2]], axis=1).reshape(2 * ntask, emb)
    wide = lambda base, count, step: jnp.concatenate(
        [sum_ref[base + a * step : base + (a + 1) * step, :] for a in range(count)], axis=1
    )
    down_ref[...] = dot_exact_tn(codes, wide(0, 64, 16))
    up_ref[...] = dot_exact_tn(codes, wide(1024, 64, 16))
    gain_ref[...] = dot_exact_tn(code, wide(2048, 12, 8))
    first_ref[...] = sum_ref[2144:2208, :]
    second_ref[...] = sum_ref[2208:2336, :emb]
    task_ref[...] = sum_ref[2336:2344, :emb]
    pos_ref[...] = sum_ref[2336:2338, emb:]


def call_rows(kernel, rows, ins, outs, scratch, cut=1, limit=60):
    def spec(item, blocked):
        if blocked is None:
            return pl.BlockSpec(memory_space=pl.ANY)
        shape = item.shape
        if blocked:
            block = (1, shape[1] // cut) + tuple(shape[2:])
            return pl.BlockSpec(block, lambda r: (r // cut, r % cut) + (0,) * (len(shape) - 2))
        return pl.BlockSpec(tuple(shape), lambda r: (0,) * len(shape))

    return pl.pallas_call(
        kernel,
        grid=(rows * cut,),
        in_specs=[spec(*item) for item in ins],
        out_specs=[spec(*item) for item in outs],
        out_shape=[item for item, _ in outs],
        scratch_shapes=scratch,
        cost_estimate=SHORT,
        compiler_params=pltpu.CompilerParams(vmem_limit_bytes=limit << 20),
    )(*[item for item, _ in ins])


def add_kernel(bits, kept_ref, got_ref, sent_ref, next_ref):
    half = sent_ref.shape[0]
    side = upper(lax.axis_index("dp"), bits)
    theirs = pl.ds(pl.multiple_of((1 - side) * half, half), half)
    mine = pl.ds(pl.multiple_of(side * half, half), half)
    sent_ref[...] = kept_ref[theirs] + got_ref[theirs]
    next_ref[...] = kept_ref[mine] + got_ref[mine]


def join_kernel(bits, cuts, own_ref, got_ref, *refs):
    *out_refs, sem = refs
    half = own_ref.shape[0]
    side = upper(lax.axis_index("dp"), bits)

    def copies(low_ref, high_ref):
        found, at = [], 0
        for cut, out_ref in zip(cuts, out_refs):
            for source, first in ((low_ref, 0), (high_ref, half)):
                low, high = max(at, first), min(at + cut, first + half)
                if low < high:
                    found.append((source.at[pl.ds(low - first, high - low)], out_ref.at[pl.ds(low - at, high - low)]))
            at += cut
        return [pltpu.make_async_copy(*pair, sem.at[i]) for i, pair in enumerate(found)]

    for place, refs in ((0, (own_ref, got_ref)), (1, (got_ref, own_ref))):

        @pl.when(side == place)
        def _():
            every = copies(*refs)
            for copy in every:
                copy.start()
            for copy in every:
                copy.wait()


def add_parts(kept, got, bits):
    half = jax.ShapeDtypeStruct((kept.shape[0] // 2,) + kept.shape[1:], f32)
    return pl.pallas_call(
        functools.partial(add_kernel, bits),
        out_shape=[half, half],
        cost_estimate=SHORT,
        compiler_params=pltpu.CompilerParams(vmem_limit_bytes=16 << 20),
    )(kept, got)


def join_parts(own, got, bits, cuts):
    any_spec = pl.BlockSpec(memory_space=pl.ANY)
    return pl.pallas_call(
        functools.partial(join_kernel, bits, cuts),
        in_specs=[any_spec] * 2,
        out_specs=[any_spec] * len(cuts),
        out_shape=[jax.ShapeDtypeStruct((cut,) + own.shape[1:], f32) for cut in cuts],
        scratch_shapes=[pltpu.SemaphoreType.DMA((2 + len(cuts),))],
        cost_estimate=SHORT,
        compiler_params=pltpu.CompilerParams(vmem_limit_bytes=1 << 20),
    )(own, got)


SEQUENCE = "10A01a0B102b2013C32011204432041323424130432132104243344D"
ORDERS = {
    "P": ((1, 1), (2, 4), (4, 2), (8, 8), (16, 16)),
    "Q": ((1, 1), (4, 2), (2, 4), (8, 8), (16, 16)),
    "R": ((1, 1), (4, 2), (8, 8), (16, 16), (2, 4)),
    "S": ((1, 1), (2, 4), (8, 8), (16, 16), (4, 2)),
}


class Line:
    def __init__(self):
        self.last = None

    def tie(self, values):
        if self.last is None:
            return values
        values, self.last["kept"] = lax.optimization_barrier((values, self.last["kept"]))
        return values


def summing(kept, sent, cuts, line, found, order):
    devices = lax.axis_size("dp")
    state = {}

    def swap(values, bits):
        moves = [(i, i ^ bits[i % 2]) for i in range(devices)]
        return lax.ppermute(values, "dp", moves)

    def mark(value):
        state["kept"] = value
        line.last = state

    high = [(32 << i, 32 << i) for i in range(max(devices // 32, 1).bit_length() - 1)]
    sent = line.tie(sent)
    got = swap(sent, order[0])
    mark(kept)
    yield
    for bits in order[1:-1]:
        got = line.tie(got)
        sent, kept = add_parts(state["kept"], got, bits)
        got = swap(sent, bits)
        mark(kept)
        yield
    for bits in list(order[-1:]) + high:
        got = line.tie(got)
        total = state["kept"] + got
        got = swap(total, bits)
        mark(total)
        yield
    got = line.tie(got)
    total = state["kept"] + got
    for bits in order[:-1][::-1]:
        got = swap(total, bits)
        mark(total)
        yield
        got = line.tie(got)
        own = state["kept"]
        if bits == order[0]:
            break
        (total,) = join_parts(own, got, bits, (2 * own.shape[0],))
    parts = join_parts(own, got, order[0], cuts)
    mark(parts[-1])
    found.append((parts[:-1], state))


def on_device(
    tokens, memory, segments, cotangent, group_sizes, task_embed, position_embed, hyper_first, hyper_second,
    hyper_gain, hyper_down, hyper_up, self_qkv, self_out, cross_qkv, cross_out, ffn_in, ffn_out,
):
    rows, seq, width = tokens.shape
    ntask = group_sizes.shape[0]
    hyper_second_t = hyper_second.T
    params = (
        task_embed, position_embed, hyper_first, hyper_second_t, hyper_gain, hyper_down, hyper_up,
        self_qkv, self_out, cross_qkv, cross_out, ffn_in, ffn_out,
    )
    (
        output, grad_two, in_kept, in_sent, out_kept, out_sent, up_two, down_two, gain_three,
        gains, down_w, up_w, pre, code, prob_one, prob_two,
        in_one, q_one, k_one, v_one, share_one, mixed_one, branch, narrow, after_one,
        in_two, q_two, k_two, v_two, share_two, mixed_two,
    ) = run_forward(tokens, memory, segments, cotangent, group_sizes, params)
    like = lambda shape, dtype=f32: jax.ShapeDtypeStruct(shape, dtype)
    wide = tokens.shape
    row_scratch = [pltpu.VMEM((seq, width), bf16)]
    total_scratch = [pltpu.VMEM((4 * width, width), f32), pltpu.SemaphoreType.DMA((2,))]
    pair = (2 * width, width)
    line = Line()
    sums = [[] for _ in range(5)]
    ff = ffn_out.shape[0]

    def start(which, kept, sent, cuts):
        return summing(kept, sent, cuts, line, sums[which], ORDERS["QQQQP"[which]])

    def mark(value):
        line.last = {"kept": value}
        return line.last

    chunks = {"0": start(0, out_kept, out_sent, (ff,)), "1": start(1, in_kept, in_sent, (width,))}
    for step in SEQUENCE:
        if step in chunks:
            next(chunks[step], None)
        elif step == "A":
            grad_two = line.tie(grad_two)
            dq, dk, dv, out_grad = call_rows(
                functools.partial(heads_back_kernel, False),
                rows,
                [
                    (grad_two, True), (mixed_two, True), (q_two, True), (k_two, True), (v_two, True),
                    (share_two, True), (prob_two, True), (cross_out, False),
                ],
                [(like(wide, bf16), True)] * 3 + [(like(cross_out.shape), False)],
                row_scratch,
            )
            held = mark(dq)
        elif step == "a":
            dq = line.tie(held["kept"])
            cross_kept, cross_sent, memory_grad, grad_one, d_branch, up_one, down_one, gain_two = call_rows(
                cross_back_kernel,
                rows,
                [
                    (grad_two, True), (dq, True), (dk, True), (dv, True), (out_grad, False), (memory, True),
                    (in_two, True), (after_one, True), (narrow, True), (branch, True),
                    (gains, False), (down_w, False), (up_w, False), (cross_qkv, False),
                ],
                [
                    (like(pair), None), (like(pair), None), (like(wide), True), (like(wide), True), (like(wide, bf16), True),
                    (like((RANK, width)), False), (like((RANK, width)), False), (like((8, width)), False),
                ],
                total_scratch,
                cut=1,
            )
            memory_grad = mark(memory_grad)
            chunks["2"] = start(2, cross_kept, cross_sent, (width, 3 * width))
        elif step == "B":
            d_branch = line.tie(d_branch)
            dq, dk, dv, out_grad = call_rows(
                functools.partial(heads_back_kernel, True),
                rows,
                [
                    (d_branch, True), (mixed_one, True), (q_one, True), (k_one, True), (v_one, True),
                    (share_one, True), (prob_one, True), (self_out, False),
                ],
                [(like(wide, bf16), True)] * 3 + [(like(self_out.shape), False)],
                row_scratch,
            )
            held = mark(dq)
        elif step == "b":
            dq = line.tie(held["kept"])
            self_kept, self_sent, input_grad, gain_one = call_rows(
                self_back_kernel,
                rows,
                [
                    (dq, True), (dk, True), (dv, True), (out_grad, False), (in_one, True), (tokens, True),
                    (grad_one, True), (gains, False), (self_qkv, False),
                ],
                [(like(pair), None), (like(pair), None), (like(wide), True), (like((8, width)), False)],
                total_scratch,
                cut=1,
            )
            input_grad = mark(input_grad)
            chunks["3"] = start(3, self_kept, self_sent, (width, 3 * width))
        elif step == "C":
            gain_one = line.tie(gain_one)
            small_kept, small_sent = pl.pallas_call(
                functools.partial(small_kernel, ntask),
                out_shape=[like((1280, LANES))] * 2,
                in_specs=[pl.BlockSpec(memory_space=pltpu.SMEM)] + [pl.BlockSpec(memory_space=pltpu.VMEM)] * 14,
                out_specs=[pl.BlockSpec(memory_space=pl.ANY)] * 2,
                scratch_shapes=[
                    pltpu.VMEM((2560, LANES), f32), pltpu.VMEM((8, 8192), f32), pltpu.VMEM((2, 64, LANES), f32),
                    pltpu.SemaphoreType.DMA((2,)),
                ],
                cost_estimate=SHORT,
        compiler_params=pltpu.CompilerParams(vmem_limit_bytes=32 << 20),
            )(
                group_sizes, up_one, up_two, down_one, down_two, gain_one, gain_two, gain_three,
                task_embed, hyper_first, hyper_second_t, hyper_gain, hyper_down, hyper_up, pre,
            )
            mark(small_kept)
            chunks["4"] = start(4, small_kept, small_sent, (2560,))
        else:
            for _ in chunks["4"]:
                pass
            sum_small = line.tie(sums[4][0][1]["kept"])
            task_grad, position_grad, first_grad, second_grad, gain_grad, down_grad, up_grad = pl.pallas_call(
                functools.partial(spread_kernel, ntask),
                out_shape=[
                    like(item.shape)
                    for item in (task_embed, position_embed, hyper_first, hyper_second, hyper_gain, hyper_down, hyper_up)
                ],
                cost_estimate=SHORT,
        compiler_params=pltpu.CompilerParams(vmem_limit_bytes=32 << 20),
            )(sum_small, code, position_embed)
            task_grad = mark(task_grad)
    for rest in chunks.values():
        for _ in rest:
            pass
    memory_grad, input_grad, task_grad = memory_grad["kept"], input_grad["kept"], task_grad["kept"]
    sum_out, sum_in, cross_qkv_grad, self_qkv_grad = (sums[i][0][1]["kept"] for i in range(4))
    cross_out_grad, self_out_grad = sums[2][0][0][0], sums[3][0][0][0]
    cross_qkv_grad = cross_qkv_grad.reshape(cross_qkv.shape)
    self_qkv_grad = self_qkv_grad.reshape(self_qkv.shape)
    return (
        output, input_grad, memory_grad, task_grad, position_grad, first_grad, second_grad, gain_grad, down_grad,
        up_grad, self_qkv_grad, self_out_grad, cross_qkv_grad, cross_out_grad, sum_in, sum_out,
    )


def solution(mesh):
    split = P("dp", None, None)
    return jax.shard_map(
        on_device,
        mesh=mesh,
        in_specs=(split, split, P("dp", None), split) + (P(),) * 14,
        out_specs=(split,) * 3 + (P(),) * 13,
        check_vma=False,
    )
```
